32 devices in a mesh: clips: 2 (over y), space: 4 (over z), tm: 2 (over x), chan: 2 (over core).
Axes of the slice: x: 2, y: 2, z: 4, core: 2. Of those that a mesh axis runs over, the one named last changes fastest.
Arguments:
- frames_in: bfloat16 [4, 16, 160, 384], P(('clips', 'tm'), 'space', None, 'chan'), parts along dimension 0, may hold values from -6 to 6
- cache: bfloat16 [4, 16, 160, 384], P('clips', 'space'), parts along dimension 0, may hold values from -6 to 6
- gain_one: bfloat16 [384], replicated, may hold values from 0.099609375 to 1.8984375
- gain_two: bfloat16 [384], replicated, may hold values from 0.099609375 to 1.8984375
- w_query: bfloat16 [384, 384], replicated, may hold values from -10 to 10
- w_key: bfloat16 [384, 384], replicated, may hold values from -10 to 10
- w_value: bfloat16 [384, 384], replicated, may hold values from -0.3125 to 0.3125
- w_out: bfloat16 [384, 384], replicated, may hold values from -0.3125 to 0.3125
- conv_weight: bfloat16 [3, 3, 3, 384, 384], P(None, None, None, None, 'chan'), may hold values from -0.0625 to 0.0625
Outputs:
- decoded: bfloat16 [4, 16, 160, 384], P(('clips', 'tm'), 'space', None, 'chan'), parts along dimension 0
The draws below stay inside these ranges and needn't reach their ends.
There are 2 independent parts, one for each index of `clips`. The reference program is written for one: setup_inputs(seed, part) draws one part's arguments, and reference() takes and returns one part's arrays. A program takes and returns all parts, laid end to end along the dimension named above; an argument that names none is the same for every part. Nothing has to cross between parts.
All inputs are finite; a program needn't handle non-finite values.
Results may differ from the reference program's by a relative error of at most 0.0062.
Values may be sent and summed in bfloat16 or wider, within the bound.
No kernel may reach another device: no remote copies, remote signals or barrier semaphores. Data moves between devices by JAX's collectives and lax.ppermute only.
A program may use at most 128 MiB of HBM per device.

```python
import math
import jax
import jax.numpy as jnp
from jax import lax

C = 384
W = 160
F = 2
H = 16


def projection_draw(key, salt):
    scatter = jax.random.truncated_normal(jax.random.fold_in(key, salt), -4.0, 4.0, (C, C), jnp.float32) / math.sqrt(C)
    return (1.75 * scatter).astype(jnp.bfloat16)


def draw_w_query(key, part):
    return projection_draw(key, 11)


def draw_w_key(key, part):
    return projection_draw(key, 13)


def draw_frames_in(key, part):
    return jax.random.truncated_normal(jax.random.fold_in(key, 25), -6.0, 6.0, (F, H, W, C), jnp.float32).astype(jnp.bfloat16)


def steps_of(stream_key, shape, pieces, smallest, high):
    level, own = 1.0, jax.random.fold_in(stream_key, 6)
    for dim, shards_of in pieces:
        draws = jnp.exp(jax.random.uniform(jax.random.fold_in(own, dim), (shards_of,), jnp.float32, smallest / len(pieces), high / len(pieces)))
        level = level * jnp.repeat(draws, shape[dim] // shards_of).reshape([-1 if axis == dim else 1 for axis in range(len(shape))])
    return level


def scatter_about(stream_key, extent, spread, most, cuts=(), held_as=jnp.bfloat16):
    entries = jax.random.normal(stream_key, extent, jnp.float32) * spread
    if len(cuts) > 0:
        entries = steps_of(stream_key, extent, cuts, -0.22, 0.18) * entries
    return jnp.clip(entries, min=-most, max=most).astype(held_as)


def setup_inputs(seed: int = 0, part: int = 0) -> dict:
    key_of = jax.random.split(jax.random.key(seed), 10)
    own_keys = jax.random.split(jax.random.fold_in(key_of[9], part), 10)
    frames_in = draw_frames_in(jax.random.fold_in(jax.random.fold_in(key_of[9], part), 71), part)
    cache = scatter_about(own_keys[1], (2, H, W, C), 1.0, 6.0, ((1, 4),))
    gain_one = jnp.clip(1.0 + 0.18 * jax.random.normal(key_of[2], (C,), jnp.float32), 0.099609375, 1.8984375).astype(jnp.bfloat16)
    gain_two = jnp.clip(1.0 + 0.18 * jax.random.normal(key_of[3], (C,), jnp.float32), 0.099609375, 1.8984375).astype(jnp.bfloat16)
    w_query = draw_w_query(jax.random.fold_in(key_of[9], 71), part)
    w_key = draw_w_key(jax.random.fold_in(key_of[9], 71), part)
    w_value = scatter_about(key_of[6], (C, C), C ** -0.5, 0.3125)
    w_out = scatter_about(key_of[7], (C, C), C ** -0.5, 0.3125)
    conv_weight = scatter_about(key_of[8], (3, 3, 3, C, C), (27 * C) ** -0.5, 0.0625, ((4, 2),))
    return dict(frames_in=frames_in, cache=cache, gain_one=gain_one, gain_two=gain_two, w_query=w_query, w_key=w_key, w_value=w_value, w_out=w_out, conv_weight=conv_weight)


def rms_scaled(values, gain):
    wide = values.astype(jnp.float32)
    factor = lax.rsqrt(lax.optimization_barrier(jnp.mean(wide * wide, axis=-1, keepdims=True)) + 1e-06)
    return wide * factor * gain.astype(jnp.float32)

def frame_attention(frame, gain_one, w_query, w_key, w_value, w_out):
    tokens = frame.reshape(-1, C)
    normed = rms_scaled(tokens, gain_one).astype(jnp.bfloat16)
    query = jnp.dot(normed, w_query, preferred_element_type=jnp.float32).astype(jnp.bfloat16)
    keys = jnp.dot(normed, w_key, preferred_element_type=jnp.float32).astype(jnp.bfloat16)
    values = jnp.dot(normed, w_value, preferred_element_type=jnp.float32).astype(jnp.bfloat16)
    block = math.gcd(tokens.shape[0], 512)
    blocks = query.reshape(-1, block, C)

    def one_block(rows):
        scores = jnp.einsum('qc,kc->qk', rows.astype(jnp.float32), keys.astype(jnp.float32)) * C ** (-0.5)
        top = lax.optimization_barrier(jnp.max(scores, axis=-1, keepdims=True))
        weights = jnp.exp(scores - top)
        total = lax.optimization_barrier(jnp.sum(weights, axis=-1, keepdims=True))
        mixed = jnp.dot(weights.astype(jnp.bfloat16), values, preferred_element_type=jnp.float32) / total
        return mixed.astype(jnp.bfloat16)
    attended = lax.map(one_block, blocks).reshape(-1, C)
    joined = tokens.astype(jnp.float32) + jnp.dot(attended, w_out, preferred_element_type=jnp.float32)
    return joined.astype(jnp.bfloat16).reshape(frame.shape)

def reference(frames_in, cache, gain_one, gain_two, w_query, w_key, w_value, w_out, conv_weight):
    joined = lax.map(lambda frame: frame_attention(frame, gain_one, w_query, w_key, w_value, w_out), frames_in)
    act = jax.nn.silu(rms_scaled(joined, gain_two)).astype(jnp.bfloat16)
    extended = jnp.concatenate([cache, act], axis=0).astype(jnp.float32)
    extended = jnp.pad(extended, ((0, 0), (1, 1), (1, 1), (0, 0)))
    conv = lax.conv_general_dilated(extended[None], conv_weight.astype(jnp.float32), (1, 1, 1), 'VALID', dimension_numbers=('NDHWC', 'DHWIO', 'NDHWC'), precision=lax.Precision.HIGHEST)[0]
    return (joined.astype(jnp.float32) + conv).astype(jnp.bfloat16)
```

```python
import functools
import math
import jax
import jax.numpy as jnp
from jax import lax
from jax.experimental import pallas as pl
from jax.experimental.pallas import tpu as pltpu
from jax.sharding import PartitionSpec as P

EPS = 1e-06
LANES = 128
BF = jnp.bfloat16
F32 = jnp.float32


def cycle(array, axis, by):
    count = lax.axis_size(axis)
    return lax.ppermute(array, axis, [(i, (i + by) % count) for i in range(count)])


def call(kernel, outs, args, scratch=(), flops=0, exps=0):
    vmem = pl.BlockSpec(memory_space=pltpu.VMEM)
    moved = sum(math.prod(a.shape) * a.dtype.itemsize for a in list(args) + list(outs))
    return pl.pallas_call(
        kernel,
        out_shape=outs,
        in_specs=[pl.BlockSpec(memory_space=pltpu.SMEM)] + [vmem] * (len(args) - 1),
        out_specs=[vmem] * len(outs),
        scratch_shapes=list(scratch),
        compiler_params=pltpu.CompilerParams(vmem_limit_bytes=36 * 2**20),
        cost_estimate=pl.CostEstimate(flops=flops, bytes_accessed=moved, transcendentals=exps),
    )(*args)


def shaped(shape, dtype):
    return jax.ShapeDtypeStruct(shape, dtype)


def dot(a, b):
    return jnp.dot(a, b, preferred_element_type=F32)


def dot_t(a, b):
    return lax.dot_general(a, b, (((1,), (1,)), ((), ())), preferred_element_type=F32)


def pack_kernel(where, x, out):
    tokens, width = x.shape
    rest = width - LANES
    out[:tokens, :] = x[:, :LANES]
    out[tokens:, :rest] = x[: tokens // 2, LANES:]
    out[tokens:, rest:] = x[tokens // 2 :, LANES:]


def joined_halves(core, mine, theirs):
    a, b = mine[...].astype(F32), theirs[...].astype(F32)
    first = jnp.where(core == 0, a, b)
    second = jnp.where(core == 0, b, a)
    tokens = a.shape[0] * 2 // 3
    low = lax.broadcasted_iota(jnp.int32, (tokens // 2, LANES), 1) < LANES // 2
    left, right = first[tokens:], second[tokens:]
    rest = jnp.concatenate(
        [
            jnp.where(low, left, pltpu.roll(right, LANES // 2, 1)),
            jnp.where(low, pltpu.roll(left, LANES // 2, 1), right),
        ],
        axis=0,
    )
    return jnp.concatenate([first[:tokens], second[:tokens], rest], axis=1)


def shuffled(array, axis):
    half = array.shape[axis] // 2
    take = lambda start, stop: lax.slice_in_dim(array, start, stop, axis=axis)
    return jnp.concatenate(
        [take(0, LANES), take(half, half + LANES), take(LANES, half), take(half + LANES, 2 * half)],
        axis=axis,
    )


def rms_scaled(wide, gain):
    factor = lax.rsqrt(jnp.mean(wide * wide, axis=-1, keepdims=True) + EPS)
    return wide * factor * gain.astype(F32)


def attend(query, keys, top, total, accum):
    scores = [dot_t(query, k) for k in keys]
    new_top = top
    for s in scores:
        most = jnp.max(s, axis=-1, keepdims=True)
        new_top = most if new_top is None else jnp.maximum(new_top, most)
    if top is not None:
        fade = jnp.exp2(top - new_top)
        total, accum = total * fade, accum * fade
    for s, k in zip(scores, keys):
        weights = jnp.exp2(s - new_top)
        part = jnp.sum(weights, axis=-1, keepdims=True)
        mixed = dot(weights.astype(BF), k)
        total = part if total is None else total + part
        accum = mixed if accum is None else accum + mixed
    return new_top, total, accum


def first_kernel(where, gain, w_query, w_key, *refs):
    core = where[0]
    tiles, (query_out, raw_out, top_out, total_out, accum_out), normed = refs[:6], refs[6:11], refs[11]
    tokens = normed.shape[1]
    edge = raw_out.shape[0] - tokens // 2
    raws = [joined_halves(core, tiles[2 * i], tiles[2 * i + 1]) for i in range(3)]
    for i in range(3):
        normed[i] = rms_scaled(raws[i], gain[...]).astype(BF)
    own, behind, ahead = raws
    half = tokens // 2
    raw_out[...] = jnp.where(
        core == 0,
        jnp.concatenate([behind[tokens - edge :], own[:half]], axis=0),
        jnp.concatenate([own[half:], ahead[:edge]], axis=0),
    ).astype(BF)
    rows = rms_scaled(raw_out[...].astype(F32), gain[...]).astype(BF)
    width = rows.shape[1]
    query = dot(rows, w_query[...]).astype(BF)
    scale = width ** (-0.5) * math.log2(math.e)
    query = (dot_t(query, w_key[...]) * scale).astype(BF)
    query_out[...] = query
    top, total, accum = attend(query, [normed[i] for i in range(3)], None, None, None)
    top_out[...] = jnp.broadcast_to(top, top_out.shape)
    total_out[...] = jnp.broadcast_to(total, total_out.shape)
    accum_out[...] = accum


def middle_kernel(count, where, gain, query, top, total, accum, *refs):
    core = where[0]
    tiles, (top_out, total_out, accum_out) = refs[: 2 * count], refs[2 * count :]
    keys = [
        rms_scaled(joined_halves(core, tiles[2 * i], tiles[2 * i + 1]), gain[...]).astype(BF)
        for i in range(count)
    ]
    new = attend(query[...], keys, top[:, :1], total[:, :1], accum[...])
    top_out[...] = jnp.broadcast_to(new[0], top_out.shape)
    total_out[...] = jnp.broadcast_to(new[1], total_out.shape)
    accum_out[...] = new[2]


def last_kernel(where, gain, gain_two, w_value, w_out, query, raw, top, total, accum, mine, theirs, act_out, joined_out):
    core, place, places = where[0], where[1], where[2]
    keys = [rms_scaled(joined_halves(core, mine, theirs), gain[...]).astype(BF)]
    _, total, accum = attend(query[...], keys, top[:, :1], total[:, :1], accum[...])
    mixed = (accum / total).astype(BF)
    attended = dot(mixed, w_value[...]).astype(BF)
    joined = (raw[...].astype(F32) + dot(attended, w_out[...])).astype(BF)
    joined_out[...] = joined
    act = rms_scaled(joined.astype(F32), gain_two[...])
    act = act / (1.0 + jnp.exp(-act))
    row = lax.broadcasted_iota(jnp.int32, (act.shape[0], 1), 0)
    edge = act.shape[0] // 3
    beyond = ((core == 0) & (place == 0) & (row < edge)) | (
        (core == 1) & (place == places - 1) & (row >= 2 * edge)
    )
    act_out[...] = jnp.where(beyond, 0.0, act).astype(BF)


def taps(padded, weights, cells):
    tokens = padded.shape[0] - 2 * cells
    wide = jnp.concatenate([padded[i * cells : i * cells + tokens] for i in range(3)], axis=1)
    return [dot(wide, weights[i]) for i in range(3)]


def gathered(parts, cells):
    left, middle, right = parts
    tokens = middle.shape[0]
    cell = lax.rem(lax.broadcasted_iota(jnp.int32, (tokens, 1), 0), cells)
    left = jnp.where(cell == 0, 0.0, pltpu.roll(left, 1, 0))
    right = jnp.where(cell == cells - 1, 0.0, pltpu.roll(right, tokens - 1, 0))
    return middle + left + right


def whole_tile(core, mine, theirs):
    a, b = mine[...], theirs[...]
    return jnp.concatenate([jnp.where(core == 0, a, b), jnp.where(core == 0, b, a)], axis=0)


def send_kernel(cells, where, act, other, weights, out):
    conv = gathered(taps(whole_tile(where[0], act, other), weights, cells), cells)
    tokens, width = conv.shape
    rest = width - LANES
    out[:tokens, :] = conv[:, :LANES].astype(BF)
    out[tokens:, :] = jnp.concatenate(
        [conv[: tokens // 2, LANES:], conv[tokens // 2 :, LANES:]], axis=1
    ).astype(BF)


def rest_kernel(cells, where, act, other, cache, halo, halo_other, w_act, w_cache, out, sums):
    core, place, places, moment = where[0], where[1], where[2], where[3]
    for i, part in enumerate(taps(whole_tile(core, act, other), w_act, cells)):
        sums[i] = part
    above = jnp.where(core == 0, halo[...], halo_other[...])
    below = jnp.where(core == 0, halo_other[...], halo[...])
    above = jnp.where(place == 0, jnp.zeros_like(above), above)
    below = jnp.where(place == places - 1, jnp.zeros_like(below), below)

    def add(frame, back):
        padded = jnp.concatenate([above[frame], cache[frame], below[frame]], axis=0)
        for i, part in enumerate(taps(padded, w_cache.at[back], cells)):
            sums[i] += part

    @pl.when(moment == 0)
    def _():
        add(0, 0)
        add(1, 1)

    @pl.when(moment == 1)
    def _():
        add(1, 0)

    out[...] = gathered([sums[i] for i in range(3)], cells)


def final_kernel(where, rest, mine, theirs, *refs):
    core, moment = where[0], where[3]
    received, out = refs[:-1], refs[-1]
    tokens, width = rest.shape
    more = width - LANES
    total = rest[...]
    for back, ref in enumerate(received):
        packed = jnp.where(moment > back, ref[...].astype(F32), 0.0)
        tail = packed[tokens:]
        tail = jnp.concatenate([tail[:, :more], tail[:, more:]], axis=0)
        total = total + jnp.concatenate([packed[:tokens], tail], axis=1)
    total = total + jnp.where(
        core == 0,
        jnp.concatenate([mine[...], theirs[...]], axis=0),
        jnp.concatenate([theirs[...], mine[...]], axis=0),
    ).astype(F32)
    out[...] = total.astype(BF)


def body(frames_in, cache, gain_one, gain_two, w_query, w_key, w_value, w_out, conv_weight):
    core, place, moment = lax.axis_index("chan"), lax.axis_index("space"), lax.axis_index("tm")
    places, moments = lax.axis_size("space"), lax.axis_size("tm")
    where = jnp.stack([core, place, jnp.int32(places), moment]).astype(jnp.int32)
    _, rows, cells, half = frames_in.shape
    tokens, width = rows * cells, 2 * half
    count = tokens // 2 + cells

    gain = shuffled(gain_one, 0).reshape(1, width)
    gain_act = shuffled(gain_two, 0).reshape(1, width)
    w_query, w_key, w_value = shuffled(w_query, 0), shuffled(w_key, 0), shuffled(w_value, 0)
    w_out = shuffled(w_out, 1)
    by_cell = conv_weight.transpose(0, 2, 1, 3, 4)
    w_cache = by_cell[:2].reshape(2, 3, 3 * width, half)
    w_act = shuffled(by_cell, 3).reshape(3, 3, 3 * width, half)

    (packed,) = call(
        pack_kernel, [shaped((tokens * 3 // 2, LANES), BF)], [where, frames_in.reshape(tokens, half)]
    )
    behind, ahead = cycle(packed, "space", 1), cycle(packed, "space", -1)
    tiles = []
    for tile in (packed, behind, ahead):
        tiles += [tile, cycle(tile, "chan", 1)]
    up, down = behind, ahead
    groups = []
    for step in range(2, places // 2 + 1):
        down = cycle(down, "space", -1)
        if 2 * step < places:
            up = cycle(up, "space", 1)
            groups.append([up, down])
        else:
            groups.append([down])

    edge = jnp.where(core == 0, cache[:, rows - 1], cache[:, 0])
    edge, down = lax.optimization_barrier((edge, down))
    groups[-1][-1] = down
    pairs = [
        (2 * i + c, 2 * ((i + 1 - 2 * c) % places) + c) for i in range(places) for c in range(2)
    ]
    halo = lax.ppermute(edge, ("space", "chan"), pairs)
    halo_other = cycle(halo, "chan", 1)

    state = [
        shaped((count, LANES), F32),
        shaped((count, LANES), F32),
        shaped((count, width), F32),
    ]
    pair_flops = 4 * count * width * tokens
    query, raw, top, total, accum = call(
        first_kernel,
        [shaped((count, width), BF), shaped((count, width), BF)] + state,
        [where, gain, w_query, w_key] + tiles,
        [pltpu.VMEM((3, tokens, width), BF)],
        flops=3 * pair_flops,
        exps=3 * count * tokens,
    )
    for group in groups[:-1]:
        tiles = []
        for tile in group:
            tiles += [tile, cycle(tile, "chan", 1)]
        top, total, accum = call(
            functools.partial(middle_kernel, len(group)),
            state,
            [where, gain, query, top, total, accum] + tiles,
            flops=len(group) * pair_flops,
            exps=len(group) * count * tokens,
        )
    tile = groups[-1][0]
    act, joined = call(
        last_kernel,
        [shaped((count, width), BF)] * 2,
        [where, gain, gain_act, w_value, w_out, query, raw, top, total, accum, tile, cycle(tile, "chan", 1)],
        flops=pair_flops + 4 * count * width * width,
        exps=count * tokens,
    )
    other = cycle(act, "chan", 1)
    kept = lax.dynamic_slice_in_dim(joined, (1 - core) * cells, tokens // 2, 0)
    lanes = lambda c: jnp.concatenate(
        [kept[:, c * LANES : (c + 1) * LANES], kept[:, 2 * LANES + c * (half - LANES) : 2 * LANES + (c + 1) * (half - LANES)]],
        axis=1,
    )
    low, high = lanes(0), lanes(1)
    mine = jnp.where(core == 0, low, high)
    theirs = cycle(jnp.where(core == 0, high, low), "chan", 1)

    conv_flops = 2 * tokens * 9 * width * half
    received = []
    for back in range(1, min(moments, 3)):
        (term,) = call(
            functools.partial(send_kernel, cells),
            [shaped((tokens * 3 // 2, LANES), BF)],
            [where, act, other, w_act[2 - back]],
            flops=conv_flops,
        )
        received.append(cycle(term, "tm", back))
    (rest,) = call(
        functools.partial(rest_kernel, cells),
        [shaped((tokens, half), F32)],
        [where, act, other, cache.reshape(2, tokens, width), halo, halo_other, w_act[2], w_cache],
        [pltpu.VMEM((3, tokens, half), F32)],
        flops=3 * conv_flops,
    )
    (out,) = call(
        final_kernel,
        [shaped((tokens, half), BF)],
        [where, rest, mine, theirs] + received,
    )
    return out.reshape(1, rows, cells, half)


def solution(mesh):
    return jax.shard_map(
        body,
        mesh=mesh,
        in_specs=(
            P(("clips", "tm"), "space", None, "chan"),
            P("clips", "space", None, None),
            P(),
            P(),
            P(),
            P(),
            P(),
            P(),
            P(None, None, None, None, "chan"),
        ),
        out_specs=P(("clips", "tm"), "space", None, "chan"),
        check_vma=False,
    )
```

```python
import functools
import math
import jax
import jax.numpy as jnp
from jax import lax
from jax.experimental import pallas as pl
from jax.experimental.pallas import tpu as pltpu
from jax.sharding import PartitionSpec as P

EPS = 1e-06
LANES = 128
BF = jnp.bfloat16
F32 = jnp.float32


def cycle(array, axis, by):
    count = lax.axis_size(axis)
    return lax.ppermute(array, axis, [(i, (i + by) % count) for i in range(count)])


def call(kernel, outs, args, scratch=(), flops=0, exps=0):
    vmem = pl.BlockSpec(memory_space=pltpu.VMEM)
    moved = sum(math.prod(a.shape) * a.dtype.itemsize for a in list(args) + list(outs))
    return pl.pallas_call(
        kernel,
        out_shape=outs,
        in_specs=[pl.BlockSpec(memory_space=pltpu.SMEM)] + [vmem] * (len(args) - 1),
        out_specs=[vmem] * len(outs),
        scratch_shapes=list(scratch),
        compiler_params=pltpu.CompilerParams(vmem_limit_bytes=36 * 2**20),
        cost_estimate=pl.CostEstimate(flops=flops, bytes_accessed=moved, transcendentals=exps),
    )(*args)


def shaped(shape, dtype):
    return jax.ShapeDtypeStruct(shape, dtype)


def dot(a, b):
    return jnp.dot(a, b, preferred_element_type=F32)


def dot_t(a, b):
    return lax.dot_general(a, b, (((1,), (1,)), ((), ())), preferred_element_type=F32)


def pack_kernel(where, x, out):
    tokens, width = x.shape
    rest = width - LANES
    out[:tokens, :] = x[:, :LANES]
    out[tokens:, :rest] = x[: tokens // 2, LANES:]
    out[tokens:, rest:] = x[tokens // 2 :, LANES:]


def joined_halves(core, mine, theirs):
    a, b = mine[...].astype(F32), theirs[...].astype(F32)
    first = jnp.where(core == 0, a, b)
    second = jnp.where(core == 0, b, a)
    tokens = a.shape[0] * 2 // 3
    turn = lambda v: pltpu.roll(v, LANES // 2, 1)
    low = lax.broadcasted_iota(jnp.int32, (tokens, LANES), 1) < LANES // 2
    middle = turn(second[:tokens])
    left = jnp.concatenate([first[tokens:], turn(first[tokens:])], axis=0)
    right = jnp.concatenate([turn(second[tokens:]), second[tokens:]], axis=0)
    return jnp.concatenate(
        [first[:tokens], jnp.where(low, left, middle), jnp.where(low, middle, right)], axis=1
    )


def rms_scaled(wide, gain):
    factor = lax.rsqrt(jnp.mean(wide * wide, axis=-1, keepdims=True) + EPS)
    return wide * factor * gain.astype(F32)


def attend(query, keys, top, total, accum):
    scores = [dot_t(query, k) for k in keys]
    new_top = top
    for s in scores:
        most = jnp.max(s, axis=-1, keepdims=True)
        new_top = most if new_top is None else jnp.maximum(new_top, most)
    if top is not None:
        fade = jnp.exp2(top - new_top)
        total, accum = total * fade, accum * fade
    for s, k in zip(scores, keys):
        weights = jnp.exp2(s - new_top)
        part = jnp.sum(weights, axis=-1, keepdims=True)
        mixed = dot(weights.astype(BF), k)
        total = part if total is None else total + part
        accum = mixed if accum is None else accum + mixed
    return new_top, total, accum


def first_kernel(where, gain, w_query, w_key, *refs):
    core = where[0]
    tiles, (query_out, raw_out, top_out, total_out, accum_out), normed = refs[:6], refs[6:11], refs[11]
    tokens = normed.shape[1]
    edge = raw_out.shape[0] - tokens // 2
    raws = [joined_halves(core, tiles[2 * i], tiles[2 * i + 1]) for i in range(3)]
    for i in range(3):
        normed[i] = rms_scaled(raws[i], gain[...]).astype(BF)
    own, behind, ahead = raws
    half = tokens // 2
    raw_out[...] = jnp.where(
        core == 0,
        jnp.concatenate([behind[tokens - edge :], own[:half]], axis=0),
        jnp.concatenate([own[half:], ahead[:edge]], axis=0),
    ).astype(BF)
    rows = rms_scaled(raw_out[...].astype(F32), gain[...]).astype(BF)
    width = rows.shape[1]
    query = dot(rows, w_query[...]).astype(BF)
    scale = width ** (-0.5) * math.log2(math.e)
    query = (dot_t(query, w_key[...]) * scale).astype(BF)
    query_out[...] = query
    top, total, accum = attend(query, [normed[i] for i in range(3)], None, None, None)
    top_out[...] = jnp.broadcast_to(top, top_out.shape)
    total_out[...] = jnp.broadcast_to(total, total_out.shape)
    accum_out[...] = accum


def middle_kernel(count, where, gain, query, top, total, accum, *refs):
    core = where[0]
    tiles, (top_out, total_out, accum_out) = refs[: 2 * count], refs[2 * count :]
    keys = [
        rms_scaled(joined_halves(core, tiles[2 * i], tiles[2 * i + 1]), gain[...]).astype(BF)
        for i in range(count)
    ]
    new = attend(query[...], keys, top[:, :1], total[:, :1], accum[...])
    top_out[...] = jnp.broadcast_to(new[0], top_out.shape)
    total_out[...] = jnp.broadcast_to(new[1], total_out.shape)
    accum_out[...] = new[2]


def last_kernel(where, gain, gain_two, w_value, w_out, query, raw, top, total, accum, mine, theirs, act_out, keep_out, give_out):
    core, place, places = where[0], where[1], where[2]
    keys = [rms_scaled(joined_halves(core, mine, theirs), gain[...]).astype(BF)]
    _, total, accum = attend(query[...], keys, top[:, :1], total[:, :1], accum[...])
    mixed = (accum / total).astype(BF)
    attended = dot(mixed, w_value[...]).astype(BF)
    joined = (raw[...].astype(F32) + dot(attended, w_out[...])).astype(BF)
    edge = joined.shape[0] // 3
    own = jnp.where(core == 0, joined[edge:], joined[: 2 * edge]).astype(F32)
    half = own.shape[1] // 2
    low, high = own[:, :half], own[:, half:]
    keep_out[...] = jnp.where(core == 0, low, high).astype(BF)
    give_out[...] = jnp.where(core == 0, high, low).astype(BF)
    act = rms_scaled(joined.astype(F32), gain_two[...])
    act = act / (1.0 + jnp.exp(-act))
    row = lax.broadcasted_iota(jnp.int32, (act.shape[0], 1), 0)
    beyond = ((core == 0) & (place == 0) & (row < edge)) | (
        (core == 1) & (place == places - 1) & (row >= 2 * edge)
    )
    act_out[...] = jnp.where(beyond, 0.0, act).astype(BF)


def taps(padded, weights, back, cells):
    tokens = padded.shape[0] - 2 * cells
    wide = jnp.concatenate([padded[i * cells : i * cells + tokens] for i in range(3)], axis=1)
    return [
        dot_t(wide, jnp.concatenate([weights[back, row, cell] for row in range(3)], axis=1))
        for cell in range(3)
    ]


def gathered(parts, cells):
    left, middle, right = parts
    tokens = middle.shape[0]
    cell = lax.rem(lax.broadcasted_iota(jnp.int32, (tokens, 1), 0), cells)
    left = jnp.where(cell == 0, 0.0, pltpu.roll(left, 1, 0))
    right = jnp.where(cell == cells - 1, 0.0, pltpu.roll(right, tokens - 1, 0))
    return middle + left + right


def whole_tile(core, mine, theirs):
    a, b = mine[...], theirs[...]
    return jnp.concatenate([jnp.where(core == 0, a, b), jnp.where(core == 0, b, a)], axis=0)


def send_kernel(cells, back, where, act, other, weights, out):
    conv = gathered(taps(whole_tile(where[0], act, other), weights, back, cells), cells)
    tokens, width = conv.shape
    rest = width - LANES
    out[:tokens, :] = conv[:, :LANES].astype(BF)
    out[tokens:, :] = jnp.concatenate(
        [conv[: tokens // 2, LANES:], conv[tokens // 2 :, LANES:]], axis=1
    ).astype(BF)


def rest_kernel(cells, where, act, other, cache, halo, halo_other, weights, out, sums):
    core, place, places, moment = where[0], where[1], where[2], where[3]
    for i, part in enumerate(taps(whole_tile(core, act, other), weights, 2, cells)):
        sums[i] = part
    above = jnp.where(core == 0, halo[...], halo_other[...])
    below = jnp.where(core == 0, halo_other[...], halo[...])
    above = jnp.where(place == 0, jnp.zeros_like(above), above)
    below = jnp.where(place == places - 1, jnp.zeros_like(below), below)

    def add(frame, back):
        padded = jnp.concatenate([above[frame], cache[frame], below[frame]], axis=0)
        for i, part in enumerate(taps(padded, weights, back, cells)):
            sums[i] += part

    @pl.when(moment == 0)
    def _():
        add(0, 0)
        add(1, 1)

    @pl.when(moment == 1)
    def _():
        add(1, 0)

    out[...] = gathered([sums[i] for i in range(3)], cells)


def final_kernel(where, rest, mine, theirs, *refs):
    core, moment = where[0], where[3]
    received, out = refs[:-1], refs[-1]
    tokens, width = rest.shape
    more = width - LANES
    total = rest[...]
    for back, ref in enumerate(received):
        packed = jnp.where(moment > back, ref[...].astype(F32), 0.0)
        tail = packed[tokens:]
        tail = jnp.concatenate([tail[:, :more], tail[:, more:]], axis=0)
        total = total + jnp.concatenate([packed[:tokens], tail], axis=1)
    total = total + jnp.where(
        core == 0,
        jnp.concatenate([mine[...], theirs[...]], axis=0),
        jnp.concatenate([theirs[...], mine[...]], axis=0),
    ).astype(F32)
    out[...] = total.astype(BF)


def body(frames_in, cache, gain_one, gain_two, w_query, w_key, w_value, w_out, conv_weight):
    core, place, moment = lax.axis_index("chan"), lax.axis_index("space"), lax.axis_index("tm")
    places, moments = lax.axis_size("space"), lax.axis_size("tm")
    where = jnp.stack([core, place, jnp.int32(places), moment]).astype(jnp.int32)
    _, rows, cells, half = frames_in.shape
    tokens, width = rows * cells, 2 * half
    count = tokens // 2 + cells

    gain = gain_one.reshape(1, width)
    gain_act = gain_two.reshape(1, width)
    weights = conv_weight.transpose(0, 1, 2, 4, 3)

    (packed,) = call(
        pack_kernel, [shaped((tokens * 3 // 2, LANES), BF)], [where, frames_in.reshape(tokens, half)]
    )
    behind, ahead = cycle(packed, "space", 1), cycle(packed, "space", -1)
    tiles = []
    for tile in (packed, behind, ahead):
        tiles += [tile, cycle(tile, "chan", 1)]
    up, down = behind, ahead
    groups = []
    for step in range(2, places // 2 + 1):
        down = cycle(down, "space", -1)
        if 2 * step < places:
            up = cycle(up, "space", 1)
            groups.append([up, down])
        else:
            groups.append([down])

    edge = jnp.where(core == 0, cache[:, rows - 1], cache[:, 0])
    edge, down = lax.optimization_barrier((edge, down))
    groups[-1][-1] = down
    pairs = [
        (2 * i + c, 2 * ((i + 1 - 2 * c) % places) + c) for i in range(places) for c in range(2)
    ]
    halo = lax.ppermute(edge, ("space", "chan"), pairs)
    halo_other = cycle(halo, "chan", 1)

    state = [
        shaped((count, LANES), F32),
        shaped((count, LANES), F32),
        shaped((count, width), F32),
    ]
    pair_flops = 4 * count * width * tokens
    query, raw, top, total, accum = call(
        first_kernel,
        [shaped((count, width), BF), shaped((count, width), BF)] + state,
        [where, gain, w_query, w_key] + tiles,
        [pltpu.VMEM((3, tokens, width), BF)],
        flops=3 * pair_flops,
        exps=3 * count * tokens,
    )
    for group in groups[:-1]:
        tiles = []
        for tile in group:
            tiles += [tile, cycle(tile, "chan", 1)]
        top, total, accum = call(
            functools.partial(middle_kernel, len(group)),
            state,
            [where, gain, query, top, total, accum] + tiles,
            flops=len(group) * pair_flops,
            exps=len(group) * count * tokens,
        )
    tile, accum = lax.optimization_barrier((groups[-1][0], accum))
    act, keep, give = call(
        last_kernel,
        [shaped((count, width), BF)] + [shaped((tokens // 2, half), BF)] * 2,
        [where, gain, gain_act, w_value, w_out, query, raw, top, total, accum, tile, cycle(tile, "chan", 1)],
        flops=pair_flops + 4 * count * width * width,
        exps=count * tokens,
    )
    other = cycle(act, "chan", 1)
    theirs = cycle(give, "chan", 1)

    conv_flops = 2 * tokens * 9 * width * half
    received = []
    for back in range(1, min(moments, 3)):
        (term,) = call(
            functools.partial(send_kernel, cells, 2 - back),
            [shaped((tokens * 3 // 2, LANES), BF)],
            [where, act, other, weights],
            flops=conv_flops,
        )
        received.append(cycle(term, "tm", back))
    (rest,) = call(
        functools.partial(rest_kernel, cells),
        [shaped((tokens, half), F32)],
        [where, act, other, cache.reshape(2, tokens, width), halo, halo_other, weights],
        [pltpu.VMEM((3, tokens, half), F32)],
        flops=3 * conv_flops,
    )
    (out,) = call(
        final_kernel,
        [shaped((tokens, half), BF)],
        [where, rest, keep, theirs] + received,
    )
    return out.reshape(1, rows, cells, half)


def solution(mesh):
    return jax.shard_map(
        body,
        mesh=mesh,
        in_specs=(
            P(("clips", "tm"), "space", None, "chan"),
            P("clips", "space", None, None),
            P(),
            P(),
            P(),
            P(),
            P(),
            P(),
            P(None, None, None, None, "chan"),
        ),
        out_specs=P(("clips", "tm"), "space", None, "chan"),
        check_vma=False,
    )
```

```python
import functools
import math
import jax
import jax.numpy as jnp
from jax import lax
from jax.experimental import pallas as pl
from jax.experimental.pallas import tpu as pltpu
from jax.sharding import PartitionSpec as P

EPS = 1e-06
LANES = 128
BF = jnp.bfloat16
F32 = jnp.float32


def cycle(array, axis, by):
    count = lax.axis_size(axis)
    return lax.ppermute(array, axis, [(i, (i + by) % count) for i in range(count)])


def between_cores(array, pieces=2):
    return jnp.concatenate([cycle(piece, "chan", 1) for piece in jnp.split(array, pieces)])


def call(kernel, outs, args, scratch=(), flops=1000):
    vmem = pl.BlockSpec(memory_space=pltpu.VMEM)
    return pl.pallas_call(
        kernel,
        out_shape=outs,
        in_specs=[pl.BlockSpec(memory_space=pltpu.SMEM)] + [vmem] * (len(args) - 1),
        out_specs=[vmem] * len(outs),
        scratch_shapes=list(scratch),
        compiler_params=pltpu.CompilerParams(vmem_limit_bytes=36 * 2**20),
        cost_estimate=pl.CostEstimate(flops=flops, bytes_accessed=1000, transcendentals=0),
    )(*args)


def shaped(shape, dtype):
    return jax.ShapeDtypeStruct(shape, dtype)


def dot(a, b):
    return jnp.dot(a, b, preferred_element_type=F32)


def dot_t(a, b):
    return lax.dot_general(a, b, (((1,), (1,)), ((), ())), preferred_element_type=F32)


def pack(x, out):
    tokens = x.shape[0]
    out[:tokens, :] = x[:, :LANES].astype(BF)
    rest = x[:, LANES:]
    out[tokens:, :] = jnp.concatenate([rest[: tokens // 2], rest[tokens // 2 :]], axis=1).astype(BF)


def unpacked(packed):
    tokens = packed.shape[0] * 2 // 3
    rest = packed[tokens:].astype(F32)
    rest = jnp.concatenate([rest[:, : LANES // 2], rest[:, LANES // 2 :]], axis=0)
    return jnp.concatenate([packed[:tokens].astype(F32), rest], axis=1)


def pack_kernel(where, x, out):
    pack(x[...], out)


def joined_halves(core, mine, theirs):
    a, b = mine[...].astype(F32), theirs[...].astype(F32)
    first = jnp.where(core == 0, a, b)
    second = jnp.where(core == 0, b, a)
    tokens = a.shape[0] * 2 // 3
    turn = lambda v: pltpu.roll(v, LANES // 2, 1)
    low = lax.broadcasted_iota(jnp.int32, (tokens, LANES), 1) < LANES // 2
    middle = turn(second[:tokens])
    left = jnp.concatenate([first[tokens:], turn(first[tokens:])], axis=0)
    right = jnp.concatenate([turn(second[tokens:]), second[tokens:]], axis=0)
    return jnp.concatenate(
        [first[:tokens], jnp.where(low, left, middle), jnp.where(low, middle, right)], axis=1
    )


def rms_scaled(wide, gain):
    factor = lax.rsqrt(jnp.mean(wide * wide, axis=-1, keepdims=True) + EPS)
    return wide * factor * gain.astype(F32)


def attend(query, keys, top, total, accum):
    scores = [dot_t(query, k) for k in keys]
    new_top = top
    for s in scores:
        most = jnp.max(s, axis=-1, keepdims=True)
        new_top = most if new_top is None else jnp.maximum(new_top, most)
    if top is not None:
        fade = jnp.exp2(top - new_top)
        total, accum = total * fade, accum * fade
    for s, k in zip(scores, keys):
        weights = jnp.exp2(s - new_top)
        part = jnp.sum(weights, axis=-1, keepdims=True)
        mixed = dot(weights.astype(BF), k)
        total = part if total is None else total + part
        accum = mixed if accum is None else accum + mixed
    return new_top, total, accum


def queries(rows, w_query, w_key):
    scale = rows.shape[1] ** (-0.5) * math.log2(math.e)
    return (dot_t(dot(rows, w_query).astype(BF), w_key) * scale).astype(BF)


def own_rows_kernel(where, gain, mine, theirs, w_query, w_key, *refs):
    raw_out, keys_out, query_out, w_query_out, w_key_out = refs
    core = where[0]
    raw = joined_halves(core, mine, theirs)
    half = raw.shape[0] // 2
    keys = rms_scaled(raw, gain[...]).astype(BF)
    keys_out[...] = keys
    raw_out[...] = jnp.where(core == 0, raw[:half], raw[half:]).astype(BF)
    rows = jnp.where(core == 0, keys[:half], keys[half:])
    query_out[...] = queries(rows, w_query[...], w_key[...])
    w_query_out[...] = w_query[...]
    w_key_out[...] = w_key[...]


def first_kernel(where, gain, raw_own, keys_own, query_own, w_query, w_key, *refs):
    core = where[0]
    tiles, (query_out, raw_out, top_out, total_out, accum_out, keys) = refs[:4], refs[4:]
    tokens = keys_own.shape[0]
    half = tokens // 2
    edge = raw_out.shape[0] - half
    behind, ahead = [joined_halves(core, tiles[2 * i], tiles[2 * i + 1]) for i in range(2)]
    keys[:tokens] = keys_own[...]
    keys[tokens : 2 * tokens] = rms_scaled(behind, gain[...]).astype(BF)
    keys[2 * tokens :] = rms_scaled(ahead, gain[...]).astype(BF)
    beyond = jnp.where(core == 0, behind[tokens - edge :], ahead[:edge])
    rows = jnp.where(core == 0, keys[2 * tokens - edge : 2 * tokens], keys[2 * tokens : 2 * tokens + edge])
    beyond = beyond.astype(BF)
    further = queries(rows, w_query[...], w_key[...])

    def ordered(own, other):
        return jnp.where(
            core == 0, jnp.concatenate([other, own], axis=0), jnp.concatenate([own, other], axis=0)
        )

    raw_out[...] = ordered(raw_own[...], beyond)
    query = ordered(query_own[...], further)
    query_out[...] = query
    top, total, accum = attend(query, [keys[...]], None, None, None)
    top_out[...] = jnp.broadcast_to(top, top_out.shape)
    total_out[...] = jnp.broadcast_to(total, total_out.shape)
    accum_out[...] = accum


def middle_kernel(count, where, gain, query, top, total, accum, *refs):
    core = where[0]
    tiles, (top_out, total_out, accum_out) = refs[: 2 * count], refs[2 * count :]
    keys = [
        rms_scaled(joined_halves(core, tiles[2 * i], tiles[2 * i + 1]), gain[...]).astype(BF)
        for i in range(count)
    ]
    new = attend(query[...], keys, top[:, :1], total[:, :1], accum[...])
    top_out[...] = jnp.broadcast_to(new[0], top_out.shape)
    total_out[...] = jnp.broadcast_to(new[1], total_out.shape)
    accum_out[...] = new[2]


def last_kernel(where, gain, gain_two, w_value, w_out, query, raw, top, total, accum, mine, theirs, act_out, keep_out, give_out):
    core, place, places = where[0], where[1], where[2]
    keys = [rms_scaled(joined_halves(core, mine, theirs), gain[...]).astype(BF)]
    _, total, accum = attend(query[...], keys, top[:, :1], total[:, :1], accum[...])
    mixed = (accum / total).astype(BF)
    attended = dot(mixed, w_value[...]).astype(BF)
    joined = (raw[...].astype(F32) + dot(attended, w_out[...])).astype(BF)
    edge = joined.shape[0] // 3
    own = jnp.where(core == 0, joined[edge:], joined[: 2 * edge]).astype(F32)
    half = own.shape[1] // 2
    low, high = own[:, :half], own[:, half:]
    keep_out[...] = jnp.where(core == 0, low, high).astype(BF)
    give_out[...] = jnp.where(core == 0, high, low).astype(BF)
    act = rms_scaled(joined.astype(F32), gain_two[...])
    act = act / (1.0 + jnp.exp(-act))
    row = lax.broadcasted_iota(jnp.int32, (act.shape[0], 1), 0)
    beyond = ((core == 0) & (place == 0) & (row < edge)) | (
        (core == 1) & (place == places - 1) & (row >= 2 * edge)
    )
    act_out[...] = jnp.where(beyond, 0.0, act).astype(BF)


def taps(padded, weights, cells):
    tokens = padded.shape[0] - 2 * cells
    wide = jnp.concatenate([padded[i * cells : i * cells + tokens] for i in range(3)], axis=1)
    return [
        dot_t(wide, jnp.concatenate([weights[row, cell] for row in range(3)], axis=1))
        for cell in range(3)
    ]


def gathered(parts, cells):
    left, middle, right = parts
    tokens = middle.shape[0]
    cell = lax.rem(lax.broadcasted_iota(jnp.int32, (tokens, 1), 0), cells)
    left = jnp.where(cell == 0, 0.0, pltpu.roll(left, 1, 0))
    right = jnp.where(cell == cells - 1, 0.0, pltpu.roll(right, tokens - 1, 0))
    return middle + left + right


def whole_tile(core, mine, theirs):
    a, b = mine[...], theirs[...]
    return jnp.concatenate([jnp.where(core == 0, a, b), jnp.where(core == 0, b, a)], axis=0)


def send_kernel(cells, back, where, act, other, weights, out):
    conv = gathered(taps(whole_tile(where[0], act, other), weights.at[back], cells), cells)
    pack(conv, out)


def cache_kernel(cells, where, cache, weights, sums, up, down):
    moment = where[3]
    tokens = cache.shape[1]
    ends = jnp.zeros((cells, cache.shape[2]), cache.dtype)

    def products(pairs):
        for i in range(3):
            sums[i] = sum(
                dot_t(
                    jnp.concatenate([padded[r * cells : r * cells + tokens] for r in range(3)], axis=1),
                    jnp.concatenate([weights[back, row, i] for row in range(3)], axis=1),
                )
                for padded, back in [
                    (jnp.concatenate([ends, cache[frame], ends], axis=0), back) for frame, back in pairs
                ]
            )
        for out, start, row in ((up, tokens - cells, 0), (down, 0, 2)):
            edge = jnp.concatenate([cache[frame, start : start + cells] for frame, _ in pairs], axis=1)
            parts = [
                dot_t(edge, jnp.concatenate([weights[back, row, i] for _, back in pairs], axis=1))
                for i in range(3)
            ]
            pack(gathered(parts, cells), out)

    @pl.when(moment == 0)
    def _():
        products([(0, 0), (1, 1)])

    @pl.when(moment == 1)
    def _():
        products([(1, 0)])

    @pl.when(moment > 1)
    def _():
        for out in (sums, up, down):
            out[...] = jnp.zeros_like(out)


def rest_kernel(cells, where, act, other, cached, weights, out):
    parts = taps(whole_tile(where[0], act, other), weights.at[2], cells)
    out[...] = gathered([part + cached[i] for i, part in enumerate(parts)], cells)


def final_kernel(cells, where, rest, mine, theirs, above, below, *refs):
    core, place, places, moment = where[0], where[1], where[2], where[3]
    received, out = refs[:-1], refs[-1]
    tokens = rest.shape[0]
    total = rest[...] + jnp.where(
        core == 0,
        jnp.concatenate([mine[...], theirs[...]], axis=0),
        jnp.concatenate([theirs[...], mine[...]], axis=0),
    ).astype(F32)
    first = jnp.where(place == 0, 0.0, unpacked(above[...]))
    last = jnp.where(place == places - 1, 0.0, unpacked(below[...]))
    total = jnp.concatenate(
        [total[:cells] + first, total[cells : tokens - cells], total[tokens - cells :] + last], axis=0
    )
    for back, ref in enumerate(received):
        total = total + jnp.where(moment > back, unpacked(ref[...]), 0.0)
    out[...] = total.astype(BF)


def body(frames_in, cache, gain_one, gain_two, w_query, w_key, w_value, w_out, conv_weight):
    core, place, moment = lax.axis_index("chan"), lax.axis_index("space"), lax.axis_index("tm")
    places, moments = lax.axis_size("space"), lax.axis_size("tm")
    where = jnp.stack([core, place, jnp.int32(places), moment]).astype(jnp.int32)
    _, rows, cells, half = frames_in.shape
    tokens, width = rows * cells, 2 * half
    count = tokens // 2 + cells

    gain = gain_one.reshape(1, width)
    gain_act = gain_two.reshape(1, width)
    weights = conv_weight.transpose(0, 1, 2, 4, 3)

    (packed,) = call(
        pack_kernel,
        [shaped((tokens * 3 // 2, LANES), BF)],
        [where, frames_in.reshape(tokens, half)],
        flops=4 * 10**9,
    )
    behind, ahead = cycle(packed, "space", 1), cycle(packed, "space", -1)
    cache = cache.reshape(2, tokens, width)
    own_other = cycle(packed, "chan", 1)
    raw_own, keys_own, query_own, w_query, w_key = call(
        own_rows_kernel,
        [
            shaped((tokens // 2, width), BF),
            shaped((tokens, width), BF),
            shaped((tokens // 2, width), BF),
            shaped((width, width), BF),
            shaped((width, width), BF),
        ],
        [where, gain, packed, own_other, w_query, w_key],
        flops=4 * 10**9,
    )
    raw_own, cache = lax.optimization_barrier((raw_own, cache))
    cached, up_term, down_term = call(
        functools.partial(cache_kernel, cells),
        [shaped((3, tokens, half), F32)] + [shaped((cells * 3 // 2, LANES), BF)] * 2,
        [where, cache, weights],
    )
    ahead, cached = lax.optimization_barrier((ahead, cached))
    ahead_other = between_cores(ahead)
    behind, ahead_other = lax.optimization_barrier((behind, ahead_other))
    tiles = [behind, between_cores(behind), ahead, ahead_other]
    up, down = behind, ahead
    groups = []
    for step in range(2, places // 2 + 1):
        down = cycle(down, "space", -1)
        if 2 * step < places:
            up = cycle(up, "space", 1)
            groups.append([up, down])
        else:
            groups.append([down])

    state = [
        shaped((count, LANES), F32),
        shaped((count, LANES), F32),
        shaped((count, width), F32),
    ]
    query, raw, top, total, accum = call(
        first_kernel,
        [shaped((count, width), BF), shaped((count, width), BF)] + state,
        [where, gain, raw_own, keys_own, query_own, w_query, w_key] + tiles,
        [pltpu.VMEM((3 * tokens, width), BF)],
    )
    for group in groups[:-1]:
        tiles = []
        for tile in group:
            tiles += [tile, cycle(tile, "chan", 1)]
        top, total, accum = call(
            functools.partial(middle_kernel, len(group)),
            state,
            [where, gain, query, top, total, accum] + tiles,
                )
    tile, accum = lax.optimization_barrier((groups[-1][0], accum))
    tile_other = between_cores(tile)
    act, keep, give = call(
        last_kernel,
        [shaped((count, width), BF)] + [shaped((tokens // 2, half), BF)] * 2,
        [where, gain, gain_act, w_value, w_out, query, raw, top, total, accum, tile, tile_other],
    )
    other = cycle(act, "chan", 1)
    theirs = cycle(give, "chan", 1)

    received = []
    for back in range(1, min(moments, 3)):
        (term,) = call(
            functools.partial(send_kernel, cells, 2 - back),
            [shaped((tokens * 3 // 2, LANES), BF)],
            [where, act, other, weights],
            )
        received.append(term)
    act, received = lax.optimization_barrier((act, received))
    received = [cycle(term, "tm", 1 + i) for i, term in enumerate(received)]
    (rest,) = call(
        functools.partial(rest_kernel, cells),
        [shaped((tokens, half), F32)],
        [where, act, other, cached, weights],
    )
    up_term, down_term, act = lax.optimization_barrier((up_term, down_term, act))
    above, below = cycle(up_term, "space", 1), cycle(down_term, "space", -1)
    (out,) = call(
        functools.partial(final_kernel, cells),
        [shaped((tokens, half), BF)],
        [where, rest, keep, theirs, above, below] + received,
    )
    return out.reshape(1, rows, cells, half)


def solution(mesh):
    return jax.shard_map(
        body,
        mesh=mesh,
        in_specs=(
            P(("clips", "tm"), "space", None, "chan"),
            P("clips", "space", None, None),
            P(),
            P(),
            P(),
            P(),
            P(),
            P(),
            P(None, None, None, None, "chan"),
        ),
        out_specs=P(("clips", "tm"), "space", None, "chan"),
        check_vma=False,
    )
```

```python
import functools
import math
import jax
import jax.numpy as jnp
from jax import lax
from jax.experimental import pallas as pl
from jax.experimental.pallas import tpu as pltpu
from jax.sharding import PartitionSpec as P

EPS = 1e-06
LANES = 128
BF = jnp.bfloat16
F32 = jnp.float32


def cycle(array, axis, by):
    count = lax.axis_size(axis)
    return lax.ppermute(array, axis, [(i, (i + by) % count) for i in range(count)])


def between_cores(array, pieces=2):
    return jnp.concatenate([cycle(piece, "chan", 1) for piece in jnp.split(array, pieces)])


def call(kernel, outs, args, scratch=(), flops=1000):
    vmem = pl.BlockSpec(memory_space=pltpu.VMEM)
    return pl.pallas_call(
        kernel,
        out_shape=outs,
        in_specs=[vmem] * len(args),
        out_specs=[vmem] * len(outs),
        scratch_shapes=list(scratch),
        compiler_params=pltpu.CompilerParams(vmem_limit_bytes=36 * 2**20),
        cost_estimate=pl.CostEstimate(flops=flops, bytes_accessed=1000, transcendentals=0),
    )(*args)


def place_of():
    return lax.axis_index("chan"), lax.axis_index("space"), lax.axis_size("space"), lax.axis_index("tm")


def shaped(shape, dtype):
    return jax.ShapeDtypeStruct(shape, dtype)


def dot(a, b):
    return jnp.dot(a, b, preferred_element_type=F32)


def dot_t(a, b):
    return lax.dot_general(a, b, (((1,), (1,)), ((), ())), preferred_element_type=F32)


def pack(x, out):
    tokens = x.shape[0]
    out[:tokens, :] = x[:, :LANES].astype(BF)
    rest = x[:, LANES:]
    out[tokens:, :] = jnp.concatenate([rest[: tokens // 2], rest[tokens // 2 :]], axis=1).astype(BF)


def unpacked(packed):
    tokens = packed.shape[0] * 2 // 3
    rest = packed[tokens:].astype(F32)
    rest = jnp.concatenate([rest[:, : LANES // 2], rest[:, LANES // 2 :]], axis=0)
    return jnp.concatenate([packed[:tokens].astype(F32), rest], axis=1)


def pack_kernel(x, out):
    pack(x[...], out)


def joined_halves(core, mine, theirs):
    a, b = mine[...].astype(F32), theirs[...].astype(F32)
    first = jnp.where(core == 0, a, b)
    second = jnp.where(core == 0, b, a)
    tokens = a.shape[0] * 2 // 3
    turn = lambda v: pltpu.roll(v, LANES // 2, 1)
    low = lax.broadcasted_iota(jnp.int32, (tokens, LANES), 1) < LANES // 2
    middle = turn(second[:tokens])
    left = jnp.concatenate([first[tokens:], turn(first[tokens:])], axis=0)
    right = jnp.concatenate([turn(second[tokens:]), second[tokens:]], axis=0)
    return jnp.concatenate(
        [first[:tokens], jnp.where(low, left, middle), jnp.where(low, middle, right)], axis=1
    )


def rms_scaled(wide, gain):
    factor = lax.rsqrt(jnp.mean(wide * wide, axis=-1, keepdims=True) + EPS)
    return wide * factor * gain.astype(F32)


def attend(query, keys, top, total, accum):
    scores = [dot_t(query, k) for k in keys]
    new_top = top
    for s in scores:
        most = jnp.max(s, axis=-1, keepdims=True)
        new_top = most if new_top is None else jnp.maximum(new_top, most)
    if top is not None:
        fade = jnp.exp2(top - new_top)
        total, accum = total * fade, accum * fade
    for s, k in zip(scores, keys):
        weights = jnp.exp2(s - new_top)
        part = jnp.sum(weights, axis=-1, keepdims=True)
        mixed = dot(weights.astype(BF), k)
        total = part if total is None else total + part
        accum = mixed if accum is None else accum + mixed
    return new_top, total, accum


def queries(rows, w_query, w_key):
    scale = rows.shape[1] ** (-0.5) * math.log2(math.e)
    return (dot_t(dot(rows, w_query).astype(BF), w_key) * scale).astype(BF)


def own_rows_kernel(gain, mine, theirs, w_query, w_key, *refs):
    raw_out, keys_out, query_out, w_query_out, w_key_out = refs
    core = place_of()[0]
    raw = joined_halves(core, mine, theirs)
    half = raw.shape[0] // 2
    keys = rms_scaled(raw, gain[...]).astype(BF)
    keys_out[...] = keys
    raw_out[...] = jnp.where(core == 0, raw[:half], raw[half:]).astype(BF)
    rows = jnp.where(core == 0, keys[:half], keys[half:])
    query_out[...] = queries(rows, w_query[...], w_key[...])
    w_query_out[...] = w_query[...]
    w_key_out[...] = w_key[...]


def first_kernel(gain, raw_own, keys_own, query_own, w_query, w_key, *refs):
    core = place_of()[0]
    tiles, (query_out, raw_out, top_out, total_out, accum_out, keys) = refs[:4], refs[4:]
    tokens = keys_own.shape[0]
    half = tokens // 2
    edge = raw_out.shape[0] - half
    behind, ahead = [joined_halves(core, tiles[2 * i], tiles[2 * i + 1]) for i in range(2)]
    keys[:tokens] = keys_own[...]
    keys[tokens : 2 * tokens] = rms_scaled(behind, gain[...]).astype(BF)
    keys[2 * tokens :] = rms_scaled(ahead, gain[...]).astype(BF)
    beyond = jnp.where(core == 0, behind[tokens - edge :], ahead[:edge])
    rows = jnp.where(core == 0, keys[2 * tokens - edge : 2 * tokens], keys[2 * tokens : 2 * tokens + edge])
    beyond = beyond.astype(BF)
    further = queries(rows, w_query[...], w_key[...])

    def ordered(own, other):
        return jnp.where(
            core == 0, jnp.concatenate([other, own], axis=0), jnp.concatenate([own, other], axis=0)
        )

    raw_out[...] = ordered(raw_own[...], beyond)
    query = ordered(query_own[...], further)
    query_out[...] = query
    top, total, accum = attend(query, [keys[...]], None, None, None)
    top_out[...] = jnp.broadcast_to(top, top_out.shape)
    total_out[...] = jnp.broadcast_to(total, total_out.shape)
    accum_out[...] = accum


def middle_kernel(count, gain, query, top, total, accum, *refs):
    core = place_of()[0]
    tiles, (top_out, total_out, accum_out) = refs[: 2 * count], refs[2 * count :]
    keys = [
        rms_scaled(joined_halves(core, tiles[2 * i], tiles[2 * i + 1]), gain[...]).astype(BF)
        for i in range(count)
    ]
    new = attend(query[...], keys, top[:, :1], total[:, :1], accum[...])
    top_out[...] = jnp.broadcast_to(new[0], top_out.shape)
    total_out[...] = jnp.broadcast_to(new[1], total_out.shape)
    accum_out[...] = new[2]


def last_kernel(gain, gain_two, w_value, w_out, query, raw, top, total, accum, mine, theirs, act_out, keep_out, give_out):
    core, place, places, _ = place_of()
    keys = [rms_scaled(joined_halves(core, mine, theirs), gain[...]).astype(BF)]
    _, total, accum = attend(query[...], keys, top[:, :1], total[:, :1], accum[...])
    mixed = (accum / total).astype(BF)
    attended = dot(mixed, w_value[...]).astype(BF)
    joined = (raw[...].astype(F32) + dot(attended, w_out[...])).astype(BF)
    edge = joined.shape[0] // 3
    own = jnp.where(core == 0, joined[edge:], joined[: 2 * edge]).astype(F32)
    half = own.shape[1] // 2
    low, high = own[:, :half], own[:, half:]
    keep_out[...] = jnp.where(core == 0, low, high).astype(BF)
    give_out[...] = jnp.where(core == 0, high, low).astype(BF)
    act = rms_scaled(joined.astype(F32), gain_two[...])
    act = act / (1.0 + jnp.exp(-act))
    row = lax.broadcasted_iota(jnp.int32, (act.shape[0], 1), 0)
    beyond = ((core == 0) & (place == 0) & (row < edge)) | (
        (core == 1) & (place == places - 1) & (row >= 2 * edge)
    )
    act_out[...] = jnp.where(beyond, 0.0, act).astype(BF)


def taps(padded, weights, cells):
    tokens = padded.shape[0] - 2 * cells
    wide = jnp.concatenate([padded[i * cells : i * cells + tokens] for i in range(3)], axis=1)
    return [
        dot_t(wide, jnp.concatenate([weights[row, cell] for row in range(3)], axis=1))
        for cell in range(3)
    ]


def gathered(parts, cells):
    left, middle, right = parts
    tokens = middle.shape[0]
    cell = lax.rem(lax.broadcasted_iota(jnp.int32, (tokens, 1), 0), cells)
    left = jnp.where(cell == 0, 0.0, pltpu.roll(left, 1, 0))
    right = jnp.where(cell == cells - 1, 0.0, pltpu.roll(right, tokens - 1, 0))
    return middle + left + right


def whole_tile(core, mine, theirs):
    a, b = mine[...], theirs[...]
    return jnp.concatenate([jnp.where(core == 0, a, b), jnp.where(core == 0, b, a)], axis=0)


def send_kernel(cells, back, act, other, weights, out):
    conv = gathered(taps(whole_tile(place_of()[0], act, other), weights.at[back], cells), cells)
    pack(conv, out)


def cache_kernel(cells, cache, weights, sums, up, down):
    moment = place_of()[3]
    tokens = cache.shape[1]
    ends = jnp.zeros((cells, cache.shape[2]), cache.dtype)

    def products(pairs):
        for i in range(3):
            sums[i] = sum(
                dot_t(
                    jnp.concatenate([padded[r * cells : r * cells + tokens] for r in range(3)], axis=1),
                    jnp.concatenate([weights[back, row, i] for row in range(3)], axis=1),
                )
                for padded, back in [
                    (jnp.concatenate([ends, cache[frame], ends], axis=0), back) for frame, back in pairs
                ]
            )
        for out, start, row in ((up, tokens - cells, 0), (down, 0, 2)):
            edge = jnp.concatenate([cache[frame, start : start + cells] for frame, _ in pairs], axis=1)
            parts = [
                dot_t(edge, jnp.concatenate([weights[back, row, i] for _, back in pairs], axis=1))
                for i in range(3)
            ]
            pack(gathered(parts, cells), out)

    @pl.when(moment == 0)
    def _():
        products([(0, 0), (1, 1)])

    @pl.when(moment == 1)
    def _():
        products([(1, 0)])

    @pl.when(moment > 1)
    def _():
        for out in (sums, up, down):
            out[...] = jnp.zeros_like(out)


def rest_kernel(cells, act, other, cached, weights, out):
    parts = taps(whole_tile(place_of()[0], act, other), weights.at[2], cells)
    out[...] = gathered([part + cached[i] for i, part in enumerate(parts)], cells)


def final_kernel(cells, rest, mine, theirs, above, below, *refs):
    core, place, places, moment = place_of()
    received, out = refs[:-1], refs[-1]
    tokens = rest.shape[0]
    total = rest[...] + jnp.where(
        core == 0,
        jnp.concatenate([mine[...], theirs[...]], axis=0),
        jnp.concatenate([theirs[...], mine[...]], axis=0),
    ).astype(F32)
    first = jnp.where(place == 0, 0.0, unpacked(above[...]))
    last = jnp.where(place == places - 1, 0.0, unpacked(below[...]))
    total = jnp.concatenate(
        [total[:cells] + first, total[cells : tokens - cells], total[tokens - cells :] + last], axis=0
    )
    for back, ref in enumerate(received):
        total = total + jnp.where(moment > back, unpacked(ref[...]), 0.0)
    out[...] = total.astype(BF)


def body(frames_in, cache, gain_one, gain_two, w_query, w_key, w_value, w_out, conv_weight):
    places, moments = lax.axis_size("space"), lax.axis_size("tm")
    _, rows, cells, half = frames_in.shape
    tokens, width = rows * cells, 2 * half
    count = tokens // 2 + cells

    gain = gain_one.reshape(1, width)
    gain_act = gain_two.reshape(1, width)
    weights = conv_weight.transpose(0, 1, 2, 4, 3)

    (packed,) = call(
        pack_kernel,
        [shaped((tokens * 3 // 2, LANES), BF)],
        [frames_in.reshape(tokens, half)],
        flops=4 * 10**9,
    )
    behind, ahead = cycle(packed, "space", 1), cycle(packed, "space", -1)
    cache = cache.reshape(2, tokens, width)
    own_other = cycle(packed, "chan", 1)
    raw_own, keys_own, query_own, w_query, w_key = call(
        own_rows_kernel,
        [
            shaped((tokens // 2, width), BF),
            shaped((tokens, width), BF),
            shaped((tokens // 2, width), BF),
            shaped((width, width), BF),
            shaped((width, width), BF),
        ],
        [gain, packed, own_other, w_query, w_key],
        flops=4 * 10**9,
    )
    raw_own, cache = lax.optimization_barrier((raw_own, cache))
    cached, up_term, down_term = call(
        functools.partial(cache_kernel, cells),
        [shaped((3, tokens, half), F32)] + [shaped((cells * 3 // 2, LANES), BF)] * 2,
        [cache, weights],
    )
    ahead, cached = lax.optimization_barrier((ahead, cached))
    ahead_other = between_cores(ahead)
    behind, ahead_other = lax.optimization_barrier((behind, ahead_other))
    tiles = [behind, between_cores(behind), ahead, ahead_other]
    up, down = behind, ahead
    groups = []
    for step in range(2, places // 2 + 1):
        down = cycle(down, "space", -1)
        if 2 * step < places:
            up = cycle(up, "space", 1)
            groups.append([up, down])
        else:
            groups.append([down])

    state = [
        shaped((count, LANES), F32),
        shaped((count, LANES), F32),
        shaped((count, width), F32),
    ]
    query, raw, top, total, accum = call(
        first_kernel,
        [shaped((count, width), BF), shaped((count, width), BF)] + state,
        [gain, raw_own, keys_own, query_own, w_query, w_key] + tiles,
        [pltpu.VMEM((3 * tokens, width), BF)],
    )
    for group in groups[:-1]:
        tiles = []
        for tile in group:
            tiles += [tile, cycle(tile, "chan", 1)]
        top, total, accum = call(
            functools.partial(middle_kernel, len(group)),
            state,
            [gain, query, top, total, accum] + tiles,
                )
    tile, accum = lax.optimization_barrier((groups[-1][0], accum))
    tile_other = between_cores(tile)
    act, keep, give = call(
        last_kernel,
        [shaped((count, width), BF)] + [shaped((tokens // 2, half), BF)] * 2,
        [gain, gain_act, w_value, w_out, query, raw, top, total, accum, tile, tile_other],
    )
    other = cycle(act, "chan", 1)
    theirs = cycle(give, "chan", 1)

    received = []
    for back in range(1, min(moments, 3)):
        (term,) = call(
            functools.partial(send_kernel, cells, 2 - back),
            [shaped((tokens * 3 // 2, LANES), BF)],
            [act, other, weights],
            )
        received.append(term)
    act, received = lax.optimization_barrier((act, received))
    received = [cycle(term, "tm", 1 + i) for i, term in enumerate(received)]
    (rest,) = call(
        functools.partial(rest_kernel, cells),
        [shaped((tokens, half), F32)],
        [act, other, cached, weights],
    )
    up_term, down_term, act = lax.optimization_barrier((up_term, down_term, act))
    above, below = cycle(up_term, "space", 1), cycle(down_term, "space", -1)
    (out,) = call(
        functools.partial(final_kernel, cells),
        [shaped((tokens, half), BF)],
        [rest, keep, theirs, above, below] + received,
    )
    return out.reshape(1, rows, cells, half)


def solution(mesh):
    return jax.shard_map(
        body,
        mesh=mesh,
        in_specs=(
            P(("clips", "tm"), "space", None, "chan"),
            P("clips", "space", None, None),
            P(),
            P(),
            P(),
            P(),
            P(),
            P(),
            P(None, None, None, None, "chan"),
        ),
        out_specs=P(("clips", "tm"), "space", None, "chan"),
        check_vma=False,
    )
```

```python
import functools
import math
import jax
import jax.numpy as jnp
from jax import lax
from jax.experimental import pallas as pl
from jax.experimental.pallas import tpu as pltpu
from jax.sharding import PartitionSpec as P

EPS = 1e-06
LANES = 128
BF = jnp.bfloat16
F32 = jnp.float32


def cycle(array, axis, by):
    count = lax.axis_size(axis)
    return lax.ppermute(array, axis, [(i, (i + by) % count) for i in range(count)])


def between_cores(array, pieces=2):
    return jnp.concatenate([cycle(piece, "chan", 1) for piece in jnp.split(array, pieces)])


def call(kernel, outs, args, scratch=(), flops=1000, kept=False):
    vmem = pl.BlockSpec(memory_space=pltpu.VMEM)
    anywhere = pl.BlockSpec(memory_space=pl.ANY)
    into = kept and args[-1].shape == outs[0].shape and args[-1].dtype == outs[0].dtype
    return pl.pallas_call(
        kernel,
        out_shape=outs,
        in_specs=[vmem] * (len(args) - into) + [anywhere] * into,
        out_specs=[anywhere if kept else vmem] * len(outs),
        input_output_aliases={len(args) - 1: 0} if into else {},
        scratch_shapes=list(scratch),
        compiler_params=pltpu.CompilerParams(vmem_limit_bytes=36 * 2**20),
        cost_estimate=pl.CostEstimate(flops=flops, bytes_accessed=1000, transcendentals=0),
    )(*args)


def place_of():
    return lax.axis_index("chan"), lax.axis_index("space"), lax.axis_size("space"), lax.axis_index("tm")


def shaped(shape, dtype):
    return jax.ShapeDtypeStruct(shape, dtype)


def dot(a, b):
    return jnp.dot(a, b, preferred_element_type=F32)


def dot_t(a, b):
    return lax.dot_general(a, b, (((1,), (1,)), ((), ())), preferred_element_type=F32)


def pack(x, out):
    tokens = x.shape[0]
    out[:tokens, :] = x[:, :LANES].astype(BF)
    rest = x[:, LANES:]
    out[tokens:, :] = jnp.concatenate([rest[: tokens // 2], rest[tokens // 2 :]], axis=1).astype(BF)


def unpacked(packed):
    tokens = packed.shape[0] * 2 // 3
    rest = packed[tokens:].astype(F32)
    rest = jnp.concatenate([rest[:, : LANES // 2], rest[:, LANES // 2 :]], axis=0)
    return jnp.concatenate([packed[:tokens].astype(F32), rest], axis=1)


def pack_kernel(x, out):
    pack(x[...], out)


def joined_halves(core, mine, theirs):
    a, b = mine[...].astype(F32), theirs[...].astype(F32)
    first = jnp.where(core == 0, a, b)
    second = jnp.where(core == 0, b, a)
    tokens = a.shape[0] * 2 // 3
    turn = lambda v: pltpu.roll(v, LANES // 2, 1)
    low = lax.broadcasted_iota(jnp.int32, (tokens, LANES), 1) < LANES // 2
    middle = turn(second[:tokens])
    left = jnp.concatenate([first[tokens:], turn(first[tokens:])], axis=0)
    right = jnp.concatenate([turn(second[tokens:]), second[tokens:]], axis=0)
    return jnp.concatenate(
        [first[:tokens], jnp.where(low, left, middle), jnp.where(low, middle, right)], axis=1
    )


def rms_scaled(wide, gain):
    factor = lax.rsqrt(jnp.mean(wide * wide, axis=-1, keepdims=True) + EPS)
    return wide * factor * gain.astype(F32)


def attend(query, keys, top, total, accum):
    scores = [dot_t(query, k) for k in keys]
    new_top = top
    for s in scores:
        most = jnp.max(s, axis=-1, keepdims=True)
        new_top = most if new_top is None else jnp.maximum(new_top, most)
    if top is not None:
        fade = jnp.exp2(top - new_top)
        total, accum = total * fade, accum * fade
    for s, k in zip(scores, keys):
        weights = jnp.exp2(s - new_top)
        part = jnp.sum(weights, axis=-1, keepdims=True)
        mixed = dot(weights.astype(BF), k)
        total = part if total is None else total + part
        accum = mixed if accum is None else accum + mixed
    return new_top, total, accum


def queries(rows, w_query, w_key):
    scale = rows.shape[1] ** (-0.5) * math.log2(math.e)
    return (dot_t(dot(rows, w_query).astype(BF), w_key) * scale).astype(BF)


def own_rows_kernel(gain, mine, theirs, w_query, w_key, w_value, w_out, *refs):
    raw_out, keys_out, query_out, w_query_out, w_key_out, w_mixed_out = refs
    core = place_of()[0]
    raw = joined_halves(core, mine, theirs)
    half = raw.shape[0] // 2
    keys = rms_scaled(raw, gain[...]).astype(BF)
    keys_out[...] = keys
    raw_out[...] = jnp.where(core == 0, raw[:half], raw[half:]).astype(BF)
    rows = jnp.where(core == 0, keys[:half], keys[half:])
    query_out[...] = queries(rows, w_query[...], w_key[...])
    w_query_out[...] = w_query[...]
    w_key_out[...] = w_key[...]
    w_mixed_out[...] = dot(w_value[...], w_out[...]).astype(BF)


def first_kernel(gain, raw_own, keys_own, query_own, w_query, w_key, *refs):
    core = place_of()[0]
    tiles, (query_out, raw_out, top_out, total_out, accum_out, keys) = refs[:4], refs[4:]
    tokens = keys_own.shape[0]
    half = tokens // 2
    edge = raw_out.shape[0] - half
    behind, ahead = [joined_halves(core, tiles[2 * i], tiles[2 * i + 1]) for i in range(2)]
    keys[:tokens] = keys_own[...]
    keys[tokens : 2 * tokens] = rms_scaled(behind, gain[...]).astype(BF)
    keys[2 * tokens :] = rms_scaled(ahead, gain[...]).astype(BF)
    beyond = jnp.where(core == 0, behind[tokens - edge :], ahead[:edge])
    rows = jnp.where(core == 0, keys[2 * tokens - edge : 2 * tokens], keys[2 * tokens : 2 * tokens + edge])
    beyond = beyond.astype(BF)
    further = queries(rows, w_query[...], w_key[...])

    def ordered(own, other):
        return jnp.where(
            core == 0, jnp.concatenate([other, own], axis=0), jnp.concatenate([own, other], axis=0)
        )

    raw_out[...] = ordered(raw_own[...], beyond)
    query = ordered(query_own[...], further)
    query_out[...] = query
    top, total, accum = attend(query, [keys[...]], None, None, None)
    top_out[...] = jnp.broadcast_to(top, top_out.shape)
    total_out[...] = jnp.broadcast_to(total, total_out.shape)
    accum_out[...] = accum


def middle_kernel(count, gain, query, top, total, accum, *refs):
    core = place_of()[0]
    tiles, (top_out, total_out, accum_out) = refs[: 2 * count], refs[2 * count :]
    keys = [
        rms_scaled(joined_halves(core, tiles[2 * i], tiles[2 * i + 1]), gain[...]).astype(BF)
        for i in range(count)
    ]
    new = attend(query[...], keys, top[:, :1], total[:, :1], accum[...])
    top_out[...] = jnp.broadcast_to(new[0], top_out.shape)
    total_out[...] = jnp.broadcast_to(new[1], total_out.shape)
    accum_out[...] = new[2]


def last_kernel(gain, gain_two, w_mixed, query, raw, top, total, accum, mine, theirs, act_out, keep_out, give_out):
    core, place, places, _ = place_of()
    keys = [rms_scaled(joined_halves(core, mine, theirs), gain[...]).astype(BF)]
    _, total, accum = attend(query[...], keys, top[:, :1], total[:, :1], accum[...])
    mixed = (accum / total).astype(BF)
    joined = (raw[...].astype(F32) + dot(mixed, w_mixed[...])).astype(BF)
    edge = joined.shape[0] // 3
    own = jnp.where(core == 0, joined[edge:], joined[: 2 * edge]).astype(F32)
    half = own.shape[1] // 2
    low, high = own[:, :half], own[:, half:]
    keep_out[...] = jnp.where(core == 0, low, high).astype(BF)
    give_out[...] = jnp.where(core == 0, high, low).astype(BF)
    act = rms_scaled(joined.astype(F32), gain_two[...])
    act = act / (1.0 + jnp.exp(-act))
    row = lax.broadcasted_iota(jnp.int32, (act.shape[0], 1), 0)
    beyond = ((core == 0) & (place == 0) & (row < edge)) | (
        (core == 1) & (place == places - 1) & (row >= 2 * edge)
    )
    act_out[...] = jnp.where(beyond, 0.0, act).astype(BF)


def taps(padded, weights, cells):
    tokens = padded.shape[0] - 2 * cells
    wide = jnp.concatenate([padded[i * cells : i * cells + tokens] for i in range(3)], axis=1)
    return [
        dot_t(wide, jnp.concatenate([weights[row, cell] for row in range(3)], axis=1))
        for cell in range(3)
    ]


def gathered(parts, cells):
    left, middle, right = parts
    tokens = middle.shape[0]
    cell = lax.rem(lax.broadcasted_iota(jnp.int32, (tokens, 1), 0), cells)
    left = jnp.where(cell == 0, 0.0, pltpu.roll(left, 1, 0))
    right = jnp.where(cell == cells - 1, 0.0, pltpu.roll(right, tokens - 1, 0))
    return middle + left + right


def by_core(mine, theirs):
    core, a, b = place_of()[0], mine[...], theirs[...]
    return jnp.concatenate([jnp.where(core == 0, a, b), jnp.where(core == 0, b, a)], axis=0)


def send_kernel(cells, back, act, other, weights, out):
    wanted = place_of()[3] + back < lax.axis_size("tm")

    @pl.when(wanted)
    def _():
        pack(gathered(taps(by_core(act, other), weights.at[2 - back], cells), cells), out)

    @pl.when(jnp.logical_not(wanted))
    def _():
        out[...] = jnp.zeros_like(out)


def cache_kernel(cells, cache, weights, sums, up, down):
    moment = place_of()[3]
    tokens = cache.shape[1]
    ends = jnp.zeros((cells, cache.shape[2]), cache.dtype)

    def products(pairs):
        for i in range(3):
            sums[i] = sum(
                dot_t(
                    jnp.concatenate([padded[r * cells : r * cells + tokens] for r in range(3)], axis=1),
                    jnp.concatenate([weights[back, row, i] for row in range(3)], axis=1),
                )
                for padded, back in [
                    (jnp.concatenate([ends, cache[frame], ends], axis=0), back) for frame, back in pairs
                ]
            )
        for out, start, row in ((up, tokens - cells, 0), (down, 0, 2)):
            edge = jnp.concatenate([cache[frame, start : start + cells] for frame, _ in pairs], axis=1)
            parts = [
                dot_t(edge, jnp.concatenate([weights[back, row, i] for _, back in pairs], axis=1))
                for i in range(3)
            ]
            pack(gathered(parts, cells), out)

    @pl.when(moment == 0)
    def _():
        products([(0, 0), (1, 1)])

    @pl.when(moment == 1)
    def _():
        products([(1, 0)])

    @pl.when(moment > 1)
    def _():
        for out in (sums, up, down):
            out[...] = jnp.zeros_like(out)


def rest_kernel(cells, act, other, cached, keep, theirs, weights, out):
    parts = taps(by_core(act, other), weights.at[2], cells)
    terms = gathered([part + cached[i] for i, part in enumerate(parts)], cells)
    out[...] = by_core(keep, theirs).astype(F32) + terms


def edge_kernel(cells, rest, above, below, out):
    _, place, places, _ = place_of()
    tokens = rest.shape[0]
    out[:cells] = rest[:cells] + jnp.where(place == 0, 0.0, unpacked(above[...]))
    out[cells : tokens - cells] = rest[cells : tokens - cells]
    out[tokens - cells :] = rest[tokens - cells :] + jnp.where(place == places - 1, 0.0, unpacked(below[...]))


def write(total, out, held, sem):
    held[...] = total.astype(BF)
    copy = pltpu.make_async_copy(held, out, sem)
    copy.start()
    copy.wait()


def early_kernel(rest, out, held, sem):
    @pl.when(place_of()[3] == 0)
    def _():
        write(rest[...], out, held, sem)


def final_kernel(rest, *refs):
    moment = place_of()[3]
    received, (_, out, held, sem) = refs[:-4], refs[-4:]

    @pl.when(moment > 0)
    def _():
        total = rest[...]
        for back, ref in enumerate(received):
            total = total + jnp.where(moment > back, unpacked(ref[...]), 0.0)
        write(total, out, held, sem)


def body(frames_in, cache, gain_one, gain_two, w_query, w_key, w_value, w_out, conv_weight):
    places, moments = lax.axis_size("space"), lax.axis_size("tm")
    _, rows, cells, half = frames_in.shape
    tokens, width = rows * cells, 2 * half
    count = tokens // 2 + cells

    gain = gain_one.reshape(1, width)
    gain_act = gain_two.reshape(1, width)
    weights = conv_weight.transpose(0, 1, 2, 4, 3)

    (packed,) = call(
        pack_kernel,
        [shaped((tokens * 3 // 2, LANES), BF)],
        [frames_in.reshape(tokens, half)],
        flops=4 * 10**9,
    )
    behind, ahead = cycle(packed, "space", 1), cycle(packed, "space", -1)
    cache = cache.reshape(2, tokens, width)
    own_other = cycle(packed, "chan", 1)
    raw_own, keys_own, query_own, w_query, w_key, w_mixed = call(
        own_rows_kernel,
        [
            shaped((tokens // 2, width), BF),
            shaped((tokens, width), BF),
            shaped((tokens // 2, width), BF),
            shaped((width, width), BF),
            shaped((width, width), BF),
            shaped((width, width), BF),
        ],
        [gain, packed, own_other, w_query, w_key, w_value, w_out],
        flops=4 * 10**9,
    )
    raw_own, cache = lax.optimization_barrier((raw_own, cache))
    cached, up_term, down_term = call(
        functools.partial(cache_kernel, cells),
        [shaped((3, tokens, half), F32)] + [shaped((cells * 3 // 2, LANES), BF)] * 2,
        [cache, weights],
    )
    ahead, cached = lax.optimization_barrier((ahead, cached))
    ahead_other = between_cores(ahead)
    behind, ahead_other = lax.optimization_barrier((behind, ahead_other))
    tiles = [behind, between_cores(behind), ahead, ahead_other]
    up, down = behind, ahead
    groups = []
    for step in range(2, places // 2 + 1):
        down = cycle(down, "space", -1)
        if 2 * step < places:
            up = cycle(up, "space", 1)
            groups.append([up, down])
        else:
            groups.append([down])

    state = [
        shaped((count, LANES), F32),
        shaped((count, LANES), F32),
        shaped((count, width), F32),
    ]
    query, raw, top, total, accum = call(
        first_kernel,
        [shaped((count, width), BF), shaped((count, width), BF)] + state,
        [gain, raw_own, keys_own, query_own, w_query, w_key] + tiles,
        [pltpu.VMEM((3 * tokens, width), BF)],
    )
    for group in groups[:-1]:
        tiles = []
        for tile in group:
            tiles += [tile, cycle(tile, "chan", 1)]
        top, total, accum = call(
            functools.partial(middle_kernel, len(group)),
            state,
            [gain, query, top, total, accum] + tiles,
                )
    tile, accum = lax.optimization_barrier((groups[-1][0], accum))
    tile_other = cycle(tile, "chan", 1)
    act, keep, give = call(
        last_kernel,
        [shaped((count, width), BF)] + [shaped((tokens // 2, half), BF)] * 2,
        [gain, gain_act, w_mixed, query, raw, top, total, accum, tile, tile_other],
    )
    other = cycle(act, "chan", 1)
    theirs = cycle(give, "chan", 1)

    received = []
    for back in range(1, min(moments, 3)):
        (term,) = call(
            functools.partial(send_kernel, cells, back),
            [shaped((tokens * 3 // 2, LANES), BF)],
            [act, other, weights],
            )
        received.append(term)
    act, received = lax.optimization_barrier((act, received))
    received = [cycle(term, "tm", 1 + i) for i, term in enumerate(received)]
    (rest,) = call(
        functools.partial(rest_kernel, cells),
        [shaped((tokens, half), F32)],
        [act, other, cached, keep, theirs, weights],
    )
    up_term, down_term, act = lax.optimization_barrier((up_term, down_term, act))
    above, below = cycle(up_term, "space", 1), cycle(down_term, "space", -1)
    (rest,) = call(
        functools.partial(edge_kernel, cells), [shaped((tokens, half), F32)], [rest, above, below]
    )
    written = [pltpu.VMEM((tokens, half), BF), pltpu.SemaphoreType.DMA]
    (out,) = call(early_kernel, [shaped((tokens, half), BF)], [rest], written, kept=True)
    (out,) = call(final_kernel, [shaped((tokens, half), BF)], [rest] + received + [out], written, kept=True)
    return out.reshape(1, rows, cells, half)


def solution(mesh):
    return jax.shard_map(
        body,
        mesh=mesh,
        in_specs=(
            P(("clips", "tm"), "space", None, "chan"),
            P("clips", "space", None, None),
            P(),
            P(),
            P(),
            P(),
            P(),
            P(),
            P(None, None, None, None, "chan"),
        ),
        out_specs=P(("clips", "tm"), "space", None, "chan"),
        check_vma=False,
    )
```

```python
import functools
import math
import jax
import jax.numpy as jnp
from jax import lax
from jax.experimental import pallas as pl
from jax.experimental.pallas import tpu as pltpu
from jax.sharding import PartitionSpec as P

EPS = 1e-06
LANES = 128
BF = jnp.bfloat16
F32 = jnp.float32


def cycle(array, axis, by):
    count = lax.axis_size(axis)
    return lax.ppermute(array, axis, [(i, (i + by) % count) for i in range(count)])


def between_cores(array, pieces=2):
    return jnp.concatenate([cycle(piece, "chan", 1) for piece in jnp.split(array, pieces)])


def call(kernel, outs, args, scratch=(), flops=1000, kept=False):
    vmem = pl.BlockSpec(memory_space=pltpu.VMEM)
    anywhere = pl.BlockSpec(memory_space=pl.ANY)
    into = kept and args[-1].shape == outs[0].shape and args[-1].dtype == outs[0].dtype
    return pl.pallas_call(
        kernel,
        out_shape=outs,
        in_specs=[vmem] * (len(args) - into) + [anywhere] * into,
        out_specs=[anywhere if kept else vmem] * len(outs),
        input_output_aliases={len(args) - 1: 0} if into else {},
        scratch_shapes=list(scratch),
        compiler_params=pltpu.CompilerParams(vmem_limit_bytes=36 * 2**20),
        cost_estimate=pl.CostEstimate(flops=flops, bytes_accessed=1000, transcendentals=0),
    )(*args)


def place_of():
    return lax.axis_index("chan"), lax.axis_index("space"), lax.axis_size("space"), lax.axis_index("tm")


def shaped(shape, dtype):
    return jax.ShapeDtypeStruct(shape, dtype)


def dot(a, b):
    return jnp.dot(a, b, preferred_element_type=F32)


def dot_t(a, b):
    return lax.dot_general(a, b, (((1,), (1,)), ((), ())), preferred_element_type=F32)


def pack(x, out):
    tokens = x.shape[0]
    out[:tokens, :] = x[:, :LANES].astype(BF)
    rest = x[:, LANES:]
    out[tokens:, :] = jnp.concatenate([rest[: tokens // 2], rest[tokens // 2 :]], axis=1).astype(BF)


def unpacked(packed):
    tokens = packed.shape[0] * 2 // 3
    rest = packed[tokens:].astype(F32)
    rest = jnp.concatenate([rest[:, : LANES // 2], rest[:, LANES // 2 :]], axis=0)
    return jnp.concatenate([packed[:tokens].astype(F32), rest], axis=1)


def pack_kernel(x, out):
    pack(x[...], out)


def joined_halves(core, mine, theirs):
    a, b = mine[...].astype(F32), theirs[...].astype(F32)
    first = jnp.where(core == 0, a, b)
    second = jnp.where(core == 0, b, a)
    tokens = a.shape[0] * 2 // 3
    turn = lambda v: pltpu.roll(v, LANES // 2, 1)
    low = lax.broadcasted_iota(jnp.int32, (tokens, LANES), 1) < LANES // 2
    middle = turn(second[:tokens])
    left = jnp.concatenate([first[tokens:], turn(first[tokens:])], axis=0)
    right = jnp.concatenate([turn(second[tokens:]), second[tokens:]], axis=0)
    return jnp.concatenate(
        [first[:tokens], jnp.where(low, left, middle), jnp.where(low, middle, right)], axis=1
    )


def rms_scaled(wide, gain):
    factor = lax.rsqrt(jnp.mean(wide * wide, axis=-1, keepdims=True) + EPS)
    return wide * factor * gain.astype(F32)


def attend(query, keys, top, total, accum):
    scores = [dot_t(query, k) for k in keys]
    new_top = top
    for s in scores:
        most = jnp.max(s, axis=-1, keepdims=True)
        new_top = most if new_top is None else jnp.maximum(new_top, most)
    if top is not None:
        fade = jnp.exp2(top - new_top)
        total, accum = total * fade, accum * fade
    for s, k in zip(scores, keys):
        weights = jnp.exp2(s - new_top)
        part = jnp.sum(weights, axis=-1, keepdims=True)
        mixed = dot(weights.astype(BF), k)
        total = part if total is None else total + part
        accum = mixed if accum is None else accum + mixed
    return new_top, total, accum


def queries(rows, w_query, w_key):
    scale = rows.shape[1] ** (-0.5) * math.log2(math.e)
    return (dot_t(dot(rows, w_query).astype(BF), w_key) * scale).astype(BF)


def own_rows_kernel(gain, mine, theirs, w_query, w_key, w_value, w_out, *refs):
    raw_out, keys_out, query_out, w_query_out, w_key_out, w_mixed_out = refs
    core = place_of()[0]
    raw = joined_halves(core, mine, theirs)
    half = raw.shape[0] // 2
    keys = rms_scaled(raw, gain[...]).astype(BF)
    keys_out[...] = keys
    raw_out[...] = jnp.where(core == 0, raw[:half], raw[half:]).astype(BF)
    rows = jnp.where(core == 0, keys[:half], keys[half:])
    query_out[...] = queries(rows, w_query[...], w_key[...])
    w_query_out[...] = w_query[...]
    w_key_out[...] = w_key[...]
    w_mixed_out[...] = dot(w_value[...], w_out[...]).astype(BF)


def first_kernel(gain, raw_own, keys_own, query_own, w_query, w_key, *refs):
    core = place_of()[0]
    tiles, (query_out, raw_out, top_out, total_out, accum_out, keys) = refs[:4], refs[4:]
    tokens = keys_own.shape[0]
    half = tokens // 2
    edge = raw_out.shape[0] - half
    behind, ahead = [joined_halves(core, tiles[2 * i], tiles[2 * i + 1]) for i in range(2)]
    keys[:tokens] = keys_own[...]
    keys[tokens : 2 * tokens] = rms_scaled(behind, gain[...]).astype(BF)
    keys[2 * tokens :] = rms_scaled(ahead, gain[...]).astype(BF)
    beyond = jnp.where(core == 0, behind[tokens - edge :], ahead[:edge])
    rows = jnp.where(core == 0, keys[2 * tokens - edge : 2 * tokens], keys[2 * tokens : 2 * tokens + edge])
    beyond = beyond.astype(BF)
    further = queries(rows, w_query[...], w_key[...])

    def ordered(own, other):
        return jnp.where(
            core == 0, jnp.concatenate([other, own], axis=0), jnp.concatenate([own, other], axis=0)
        )

    raw_out[...] = ordered(raw_own[...], beyond)
    query = ordered(query_own[...], further)
    query_out[...] = query
    top, total, accum = attend(query, [keys[...]], None, None, None)
    top_out[...] = jnp.broadcast_to(top, top_out.shape)
    total_out[...] = jnp.broadcast_to(total, total_out.shape)
    accum_out[...] = accum


def middle_kernel(count, gain, query, top, total, accum, *refs):
    core = place_of()[0]
    tiles, (top_out, total_out, accum_out) = refs[: 2 * count], refs[2 * count :]
    keys = [
        rms_scaled(joined_halves(core, tiles[2 * i], tiles[2 * i + 1]), gain[...]).astype(BF)
        for i in range(count)
    ]
    new = attend(query[...], keys, top[:, :1], total[:, :1], accum[...])
    top_out[...] = jnp.broadcast_to(new[0], top_out.shape)
    total_out[...] = jnp.broadcast_to(new[1], total_out.shape)
    accum_out[...] = new[2]


def last_kernel(gain, gain_two, w_mixed, query, raw, top, total, accum, mine, theirs, *refs):
    core, place, places, _ = place_of()
    act_out, keep_out, give_out, total_now, accum_now = refs
    keys = rms_scaled(joined_halves(core, mine, theirs), gain[...]).astype(BF)
    scores = dot_t(query[...], keys) - top[:, :1]
    weights = jnp.exp2(scores)
    total_now[...] = total[:, :1] + jnp.sum(weights, axis=-1, keepdims=True)
    accum_now[...] = accum[...] + dot(weights.astype(BF), keys)

    @pl.when(jnp.max(scores) > 60.0)
    def _():
        _, total_now[...], accum_now[...] = attend(query[...], [keys], top[:, :1], total[:, :1], accum[...])

    mixed = (accum_now[...] / total_now[...]).astype(BF)
    joined = (raw[...].astype(F32) + dot(mixed, w_mixed[...])).astype(BF)
    edge = joined.shape[0] // 3
    own = jnp.where(core == 0, joined[edge:], joined[: 2 * edge]).astype(F32)
    half = own.shape[1] // 2
    low, high = own[:, :half], own[:, half:]
    keep_out[...] = jnp.where(core == 0, low, high).astype(BF)
    give_out[...] = jnp.where(core == 0, high, low).astype(BF)
    act = rms_scaled(joined.astype(F32), gain_two[...])
    act = act / (1.0 + jnp.exp(-act))
    row = lax.broadcasted_iota(jnp.int32, (act.shape[0], 1), 0)
    beyond = ((core == 0) & (place == 0) & (row < edge)) | (
        (core == 1) & (place == places - 1) & (row >= 2 * edge)
    )
    act_out[...] = jnp.where(beyond, 0.0, act).astype(BF)


def taps(padded, weights, cells):
    tokens = padded.shape[0] - 2 * cells
    wide = jnp.concatenate([padded[i * cells : i * cells + tokens] for i in range(3)], axis=1)
    return [
        dot_t(wide, jnp.concatenate([weights[row, cell] for row in range(3)], axis=1))
        for cell in range(3)
    ]


def gathered(parts, cells):
    left, middle, right = parts
    tokens = middle.shape[0]
    cell = lax.rem(lax.broadcasted_iota(jnp.int32, (tokens, 1), 0), cells)
    left = jnp.where(cell == 0, 0.0, pltpu.roll(left, 1, 0))
    right = jnp.where(cell == cells - 1, 0.0, pltpu.roll(right, tokens - 1, 0))
    return middle + left + right


def by_core(mine, theirs):
    core, a, b = place_of()[0], mine[...], theirs[...]
    return jnp.concatenate([jnp.where(core == 0, a, b), jnp.where(core == 0, b, a)], axis=0)


def send_kernel(cells, back, act, other, weights, out):
    wanted = place_of()[3] + back < lax.axis_size("tm")

    @pl.when(wanted)
    def _():
        pack(gathered(taps(by_core(act, other), weights.at[2 - back], cells), cells), out)

    @pl.when(jnp.logical_not(wanted))
    def _():
        out[...] = jnp.zeros_like(out)


def cache_kernel(cells, cache, weights, sums, inner, outer):
    _, place, _, moment = place_of()
    tokens = cache.shape[1]
    ends = jnp.zeros((cells, cache.shape[2]), cache.dtype)

    def products(pairs):
        for i in range(3):
            sums[i] = sum(
                dot_t(
                    jnp.concatenate([padded[r * cells : r * cells + tokens] for r in range(3)], axis=1),
                    jnp.concatenate([weights[back, row, i] for row in range(3)], axis=1),
                )
                for padded, back in [
                    (jnp.concatenate([ends, cache[frame], ends], axis=0), back) for frame, back in pairs
                ]
            )
        finished = []
        for start, row in ((tokens - cells, 0), (0, 2)):
            edge = jnp.concatenate([cache[frame, start : start + cells] for frame, _ in pairs], axis=1)
            parts = [
                dot_t(edge, jnp.concatenate([weights[back, row, i] for _, back in pairs], axis=1))
                for i in range(3)
            ]
            finished.append(gathered(parts, cells))
        up, down = finished
        even = lax.rem(place, 2) == 0
        pack(jnp.where(even, up, down), inner)
        pack(jnp.where(even, down, up), outer)

    @pl.when(moment == 0)
    def _():
        products([(0, 0), (1, 1)])

    @pl.when(moment == 1)
    def _():
        products([(1, 0)])

    @pl.when(moment > 1)
    def _():
        for out in (sums, inner, outer):
            out[...] = jnp.zeros_like(out)


def rest_kernel(cells, act, other, cached, keep, theirs, weights, out):
    parts = taps(by_core(act, other), weights.at[2], cells)
    terms = gathered([part + cached[i] for i, part in enumerate(parts)], cells)
    out[...] = by_core(keep, theirs).astype(F32) + terms


def edge_kernel(cells, rest, outer, inner, out):
    _, place, places, _ = place_of()
    tokens = rest.shape[0]
    even = lax.rem(place, 2) == 0
    above, below = jnp.where(even, outer[...], inner[...]), jnp.where(even, inner[...], outer[...])
    out[:cells] = rest[:cells] + jnp.where(place == 0, 0.0, unpacked(above))
    out[cells : tokens - cells] = rest[cells : tokens - cells]
    out[tokens - cells :] = rest[tokens - cells :] + jnp.where(place == places - 1, 0.0, unpacked(below))


def write(total, out, held, sem):
    held[...] = total.astype(BF)
    copy = pltpu.make_async_copy(held, out, sem)
    copy.start()
    copy.wait()


def early_kernel(rest, out, held, sem):
    @pl.when(place_of()[3] == 0)
    def _():
        write(rest[...], out, held, sem)


def final_kernel(rest, *refs):
    moment = place_of()[3]
    received, (_, out, held, sem) = refs[:-4], refs[-4:]

    @pl.when(moment > 0)
    def _():
        total = rest[...]
        for back, ref in enumerate(received):
            total = total + jnp.where(moment > back, unpacked(ref[...]), 0.0)
        write(total, out, held, sem)


def body(frames_in, cache, gain_one, gain_two, w_query, w_key, w_value, w_out, conv_weight):
    places, moments = lax.axis_size("space"), lax.axis_size("tm")
    _, rows, cells, half = frames_in.shape
    tokens, width = rows * cells, 2 * half
    count = tokens // 2 + cells

    gain = gain_one.reshape(1, width)
    gain_act = gain_two.reshape(1, width)
    weights = conv_weight.transpose(0, 1, 2, 4, 3)

    (packed,) = call(
        pack_kernel,
        [shaped((tokens * 3 // 2, LANES), BF)],
        [frames_in.reshape(tokens, half)],
        flops=4 * 10**9,
    )
    behind, ahead = cycle(packed, "space", 1), cycle(packed, "space", -1)
    cache = cache.reshape(2, tokens, width)
    own_other = between_cores(packed)
    raw_own, keys_own, query_own, w_query, w_key, w_mixed = call(
        own_rows_kernel,
        [
            shaped((tokens // 2, width), BF),
            shaped((tokens, width), BF),
            shaped((tokens // 2, width), BF),
            shaped((width, width), BF),
            shaped((width, width), BF),
            shaped((width, width), BF),
        ],
        [gain, packed, own_other, w_query, w_key, w_value, w_out],
        flops=1000,
    )
    raw_own, cache = lax.optimization_barrier((raw_own, cache))
    cached, inner, outer = call(
        functools.partial(cache_kernel, cells),
        [shaped((3, tokens, half), F32)] + [shaped((cells * 3 // 2, LANES), BF)] * 2,
        [cache, weights],
    )
    ahead, cached = lax.optimization_barrier((ahead, cached))
    ahead_other = between_cores(ahead)
    behind, ahead_other = lax.optimization_barrier((behind, ahead_other))
    tiles = [behind, between_cores(behind), ahead, ahead_other]
    up, down = behind, ahead
    groups = []
    for step in range(2, places // 2 + 1):
        down = cycle(down, "space", -1)
        if 2 * step < places:
            up = cycle(up, "space", 1)
            groups.append([up, down])
        else:
            groups.append([down])

    state = [
        shaped((count, LANES), F32),
        shaped((count, LANES), F32),
        shaped((count, width), F32),
    ]
    query, raw, top, total, accum = call(
        first_kernel,
        [shaped((count, width), BF), shaped((count, width), BF)] + state,
        [gain, raw_own, keys_own, query_own, w_query, w_key] + tiles,
        [pltpu.VMEM((3 * tokens, width), BF)],
    )
    for group in groups[:-1]:
        tiles = []
        for tile in group:
            tiles += [tile, cycle(tile, "chan", 1)]
        top, total, accum = call(
            functools.partial(middle_kernel, len(group)),
            state,
            [gain, query, top, total, accum] + tiles,
                )
    tile, accum = lax.optimization_barrier((groups[-1][0], accum))
    tile_other = cycle(tile, "chan", 1)
    act, keep, give = call(
        last_kernel,
        [shaped((count, width), BF)] + [shaped((tokens // 2, half), BF)] * 2,
        [gain, gain_act, w_mixed, query, raw, top, total, accum, tile, tile_other],
        [pltpu.VMEM((count, 1), F32), pltpu.VMEM((count, width), F32)],
    )
    other = cycle(act, "chan", 1)
    theirs = cycle(give, "chan", 1)

    received = []
    for back in range(1, min(moments, 3)):
        (term,) = call(
            functools.partial(send_kernel, cells, back),
            [shaped((tokens * 3 // 2, LANES), BF)],
            [act, other, weights],
            )
        received.append(term)
    act, received = lax.optimization_barrier((act, received))
    received = [cycle(term, "tm", 1 + i) for i, term in enumerate(received)]
    (rest,) = call(
        functools.partial(rest_kernel, cells),
        [shaped((tokens, half), F32)],
        [act, other, cached, keep, theirs, weights],
    )
    inner, outer, act = lax.optimization_barrier((inner, outer, act))
    outer = lax.ppermute(
        outer, "space", [(i, min(max(((i + 1) ^ 1) - 1, 0), places - 1)) for i in range(places)]
    )
    inner = lax.ppermute(inner, "space", [(i, i ^ 1) for i in range(places)])
    (rest,) = call(
        functools.partial(edge_kernel, cells), [shaped((tokens, half), F32)], [rest, outer, inner]
    )
    written = [pltpu.VMEM((tokens, half), BF), pltpu.SemaphoreType.DMA]
    (out,) = call(early_kernel, [shaped((tokens, half), BF)], [rest], written, kept=True)
    (out,) = call(final_kernel, [shaped((tokens, half), BF)], [rest] + received + [out], written, kept=True)
    return out.reshape(1, rows, cells, half)


def solution(mesh):
    return jax.shard_map(
        body,
        mesh=mesh,
        in_specs=(
            P(("clips", "tm"), "space", None, "chan"),
            P("clips", "space", None, None),
            P(),
            P(),
            P(),
            P(),
            P(),
            P(),
            P(None, None, None, None, "chan"),
        ),
        out_specs=P(("clips", "tm"), "space", None, "chan"),
        check_vma=False,
    )
```

```python
import functools
import math
import jax
import jax.numpy as jnp
from jax import lax
from jax.experimental import pallas as pl
from jax.experimental.pallas import tpu as pltpu
from jax.sharding import PartitionSpec as P

EPS = 1e-06
LANES = 128
BF = jnp.bfloat16
F32 = jnp.float32


def cycle(array, axis, by):
    count = lax.axis_size(axis)
    return lax.ppermute(array, axis, [(i, (i + by) % count) for i in range(count)])


def between_cores(array, pieces=2):
    return jnp.concatenate([cycle(piece, "chan", 1) for piece in jnp.split(array, pieces)])


def call(kernel, outs, args, scratch=(), flops=1000, kept=False):
    vmem = pl.BlockSpec(memory_space=pltpu.VMEM)
    anywhere = pl.BlockSpec(memory_space=pl.ANY)
    into = kept and args[-1].shape == outs[0].shape and args[-1].dtype == outs[0].dtype
    return pl.pallas_call(
        kernel,
        out_shape=outs,
        in_specs=[vmem] * (len(args) - into) + [anywhere] * into,
        out_specs=[anywhere if kept else vmem] * len(outs),
        input_output_aliases={len(args) - 1: 0} if into else {},
        scratch_shapes=list(scratch),
        compiler_params=pltpu.CompilerParams(vmem_limit_bytes=36 * 2**20),
        cost_estimate=pl.CostEstimate(flops=flops, bytes_accessed=1000, transcendentals=0),
    )(*args)


def place_of():
    return lax.axis_index("chan"), lax.axis_index("space"), lax.axis_size("space"), lax.axis_index("tm")


def shaped(shape, dtype):
    return jax.ShapeDtypeStruct(shape, dtype)


def dot(a, b):
    return jnp.dot(a, b, preferred_element_type=F32)


def dot_t(a, b):
    return lax.dot_general(a, b, (((1,), (1,)), ((), ())), preferred_element_type=F32)


def pack(x, out):
    tokens = x.shape[0]
    out[:tokens, :] = x[:, :LANES].astype(BF)
    rest = x[:, LANES:]
    out[tokens:, :] = jnp.concatenate([rest[: tokens // 2], rest[tokens // 2 :]], axis=1).astype(BF)


def unpacked(packed):
    tokens = packed.shape[0] * 2 // 3
    rest = packed[tokens:].astype(F32)
    rest = jnp.concatenate([rest[:, : LANES // 2], rest[:, LANES // 2 :]], axis=0)
    return jnp.concatenate([packed[:tokens].astype(F32), rest], axis=1)


def pack_kernel(x, out):
    pack(x[...], out)


def joined_halves(core, mine, theirs):
    a, b = mine[...].astype(F32), theirs[...].astype(F32)
    first = jnp.where(core == 0, a, b)
    second = jnp.where(core == 0, b, a)
    tokens = a.shape[0] * 2 // 3
    turn = lambda v: pltpu.roll(v, LANES // 2, 1)
    low = lax.broadcasted_iota(jnp.int32, (tokens, LANES), 1) < LANES // 2
    middle = turn(second[:tokens])
    left = jnp.concatenate([first[tokens:], turn(first[tokens:])], axis=0)
    right = jnp.concatenate([turn(second[tokens:]), second[tokens:]], axis=0)
    return jnp.concatenate(
        [first[:tokens], jnp.where(low, left, middle), jnp.where(low, middle, right)], axis=1
    )


def rms_scaled(wide, gain):
    factor = lax.rsqrt(jnp.mean(wide * wide, axis=-1, keepdims=True) + EPS)
    return wide * factor * gain.astype(F32)


def attend(query, keys, top, total, accum):
    scores = [dot_t(query, k) for k in keys]
    new_top = top
    for s in scores:
        most = jnp.max(s, axis=-1, keepdims=True)
        new_top = most if new_top is None else jnp.maximum(new_top, most)
    if top is not None:
        fade = jnp.exp2(top - new_top)
        total, accum = total * fade, accum * fade
    for s, k in zip(scores, keys):
        weights = jnp.exp2(s - new_top)
        part = jnp.sum(weights, axis=-1, keepdims=True)
        mixed = dot(weights.astype(BF), k)
        total = part if total is None else total + part
        accum = mixed if accum is None else accum + mixed
    return new_top, total, accum


def queries(rows, w_query, w_key):
    scale = rows.shape[1] ** (-0.5) * math.log2(math.e)
    return (dot_t(dot(rows, w_query).astype(BF), w_key) * scale).astype(BF)


def own_rows_kernel(gain, mine, theirs, w_query, w_key, w_value, w_out, *refs):
    raw_out, keys_out, query_out, w_query_out, w_key_out, w_mixed_out = refs
    core = place_of()[0]
    raw = joined_halves(core, mine, theirs)
    half = raw.shape[0] // 2
    keys = rms_scaled(raw, gain[...]).astype(BF)
    keys_out[...] = keys
    raw_out[...] = jnp.where(core == 0, raw[:half], raw[half:]).astype(BF)
    rows = jnp.where(core == 0, keys[:half], keys[half:])
    query_out[...] = queries(rows, w_query[...], w_key[...])
    w_query_out[...] = w_query[...]
    w_key_out[...] = w_key[...]
    w_mixed_out[...] = dot(w_value[...], w_out[...]).astype(BF)


def first_kernel(gain, raw_own, keys_own, query_own, w_query, w_key, *refs):
    core = place_of()[0]
    tiles, (query_out, raw_out, top_out, total_out, accum_out, keys) = refs[:4], refs[4:]
    tokens = keys_own.shape[0]
    half = tokens // 2
    edge = raw_out.shape[0] - half
    behind, ahead = [joined_halves(core, tiles[2 * i], tiles[2 * i + 1]) for i in range(2)]
    keys[:tokens] = keys_own[...]
    keys[tokens : 2 * tokens] = rms_scaled(behind, gain[...]).astype(BF)
    keys[2 * tokens :] = rms_scaled(ahead, gain[...]).astype(BF)
    beyond = jnp.where(core == 0, behind[tokens - edge :], ahead[:edge])
    rows = jnp.where(core == 0, keys[2 * tokens - edge : 2 * tokens], keys[2 * tokens : 2 * tokens + edge])
    beyond = beyond.astype(BF)
    further = queries(rows, w_query[...], w_key[...])

    def ordered(own, other):
        return jnp.where(
            core == 0, jnp.concatenate([other, own], axis=0), jnp.concatenate([own, other], axis=0)
        )

    raw_out[...] = ordered(raw_own[...], beyond)
    query = ordered(query_own[...], further)
    query_out[...] = query
    top, total, accum = attend(query, [keys[...]], None, None, None)
    top_out[...] = jnp.broadcast_to(top, top_out.shape)
    total_out[...] = jnp.broadcast_to(total, total_out.shape)
    accum_out[...] = accum


def middle_kernel(count, gain, query, top, total, accum, *refs):
    core = place_of()[0]
    tiles, (top_out, total_out, accum_out) = refs[: 2 * count], refs[2 * count :]
    keys = [
        rms_scaled(joined_halves(core, tiles[2 * i], tiles[2 * i + 1]), gain[...]).astype(BF)
        for i in range(count)
    ]
    new = attend(query[...], keys, top[:, :1], total[:, :1], accum[...])
    top_out[...] = jnp.broadcast_to(new[0], top_out.shape)
    total_out[...] = jnp.broadcast_to(new[1], total_out.shape)
    accum_out[...] = new[2]


def last_kernel(gain, gain_two, w_mixed, query, raw, top, total, accum, mine, theirs, *refs):
    core, place, places, _ = place_of()
    act_out, joined_out, total_now, accum_now = refs
    keys = rms_scaled(joined_halves(core, mine, theirs), gain[...]).astype(BF)
    scores = dot_t(query[...], keys) - top[:, :1]
    weights = jnp.exp2(scores)
    total_now[...] = total[:, :1] + jnp.sum(weights, axis=-1, keepdims=True)
    accum_now[...] = accum[...] + dot(weights.astype(BF), keys)

    @pl.when(jnp.max(scores) > 60.0)
    def _():
        _, total_now[...], accum_now[...] = attend(query[...], [keys], top[:, :1], total[:, :1], accum[...])

    mixed = (accum_now[...] / total_now[...]).astype(BF)
    joined = (raw[...].astype(F32) + dot(mixed, w_mixed[...])).astype(BF)
    joined_out[...] = joined
    edge = joined.shape[0] // 3
    act = rms_scaled(joined.astype(F32), gain_two[...])
    act = act / (1.0 + jnp.exp(-act))
    row = lax.broadcasted_iota(jnp.int32, (act.shape[0], 1), 0)
    beyond = ((core == 0) & (place == 0) & (row < edge)) | (
        (core == 1) & (place == places - 1) & (row >= 2 * edge)
    )
    act_out[...] = jnp.where(beyond, 0.0, act).astype(BF)


def residual_kernel(joined, keep_out, give_out):
    core = place_of()[0]
    edge = joined.shape[0] // 3
    own = jnp.where(core == 0, joined[edge:], joined[: 2 * edge]).astype(F32)
    half = own.shape[1] // 2
    low, high = own[:, :half], own[:, half:]
    keep_out[...] = jnp.where(core == 0, low, high).astype(BF)
    give_out[...] = jnp.where(core == 0, high, low).astype(BF)


def taps(padded, weights, cells):
    tokens = padded.shape[0] - 2 * cells
    wide = jnp.concatenate([padded[i * cells : i * cells + tokens] for i in range(3)], axis=1)
    return [
        dot_t(wide, jnp.concatenate([weights[row, cell] for row in range(3)], axis=1))
        for cell in range(3)
    ]


def gathered(parts, cells):
    left, middle, right = parts
    tokens = middle.shape[0]
    cell = lax.rem(lax.broadcasted_iota(jnp.int32, (tokens, 1), 0), cells)
    left = jnp.where(cell == 0, 0.0, pltpu.roll(left, 1, 0))
    right = jnp.where(cell == cells - 1, 0.0, pltpu.roll(right, tokens - 1, 0))
    return middle + left + right


def by_core(mine, theirs):
    core, a, b = place_of()[0], mine[...], theirs[...]
    return jnp.concatenate([jnp.where(core == 0, a, b), jnp.where(core == 0, b, a)], axis=0)


def send_kernel(cells, back, act, other, weights, out):
    wanted = place_of()[3] + back < lax.axis_size("tm")

    @pl.when(wanted)
    def _():
        pack(gathered(taps(by_core(act, other), weights.at[2 - back], cells), cells), out)

    @pl.when(jnp.logical_not(wanted))
    def _():
        out[...] = jnp.zeros_like(out)


def cache_kernel(cells, cache, weights, sums, inner, outer):
    _, place, _, moment = place_of()
    tokens = cache.shape[1]
    ends = jnp.zeros((cells, cache.shape[2]), cache.dtype)

    def products(pairs):
        for i in range(3):
            sums[i] = sum(
                dot_t(
                    jnp.concatenate([padded[r * cells : r * cells + tokens] for r in range(3)], axis=1),
                    jnp.concatenate([weights[back, row, i] for row in range(3)], axis=1),
                )
                for padded, back in [
                    (jnp.concatenate([ends, cache[frame], ends], axis=0), back) for frame, back in pairs
                ]
            )
        finished = []
        for start, row in ((tokens - cells, 0), (0, 2)):
            edge = jnp.concatenate([cache[frame, start : start + cells] for frame, _ in pairs], axis=1)
            parts = [
                dot_t(edge, jnp.concatenate([weights[back, row, i] for _, back in pairs], axis=1))
                for i in range(3)
            ]
            finished.append(gathered(parts, cells))
        up, down = finished
        even = lax.rem(place, 2) == 0
        pack(jnp.where(even, up, down), inner)
        pack(jnp.where(even, down, up), outer)

    @pl.when(moment == 0)
    def _():
        products([(0, 0), (1, 1)])

    @pl.when(moment == 1)
    def _():
        products([(1, 0)])

    @pl.when(moment > 1)
    def _():
        for out in (sums, inner, outer):
            out[...] = jnp.zeros_like(out)


def rest_kernel(cells, act, other, cached, keep, theirs, weights, out):
    parts = taps(by_core(act, other), weights.at[2], cells)
    terms = gathered([part + cached[i] for i, part in enumerate(parts)], cells)
    out[...] = by_core(keep, theirs).astype(F32) + terms


def edge_kernel(cells, rest, outer, inner, out):
    _, place, places, _ = place_of()
    tokens = rest.shape[0]
    even = lax.rem(place, 2) == 0
    above, below = jnp.where(even, outer[...], inner[...]), jnp.where(even, inner[...], outer[...])
    out[:cells] = rest[:cells] + jnp.where(place == 0, 0.0, unpacked(above))
    out[cells : tokens - cells] = rest[cells : tokens - cells]
    out[tokens - cells :] = rest[tokens - cells :] + jnp.where(place == places - 1, 0.0, unpacked(below))


def write(total, out, held, sem):
    held[...] = total.astype(BF)
    copy = pltpu.make_async_copy(held, out, sem)
    copy.start()
    copy.wait()


def early_kernel(rest, out, held, sem):
    @pl.when(place_of()[3] == 0)
    def _():
        write(rest[...], out, held, sem)


def final_kernel(rest, *refs):
    moment = place_of()[3]
    received, (_, out, held, sem) = refs[:-4], refs[-4:]

    @pl.when(moment > 0)
    def _():
        total = rest[...]
        for back, ref in enumerate(received):
            total = total + jnp.where(moment > back, unpacked(ref[...]), 0.0)
        write(total, out, held, sem)


def body(frames_in, cache, gain_one, gain_two, w_query, w_key, w_value, w_out, conv_weight):
    places, moments = lax.axis_size("space"), lax.axis_size("tm")
    _, rows, cells, half = frames_in.shape
    tokens, width = rows * cells, 2 * half
    count = tokens // 2 + cells

    gain = gain_one.reshape(1, width)
    gain_act = gain_two.reshape(1, width)
    weights = conv_weight.transpose(0, 1, 2, 4, 3)

    (packed,) = call(
        pack_kernel,
        [shaped((tokens * 3 // 2, LANES), BF)],
        [frames_in.reshape(tokens, half)],
        flops=4 * 10**9,
    )
    behind, ahead = cycle(packed, "space", 1), cycle(packed, "space", -1)
    cache = cache.reshape(2, tokens, width)
    own_other = between_cores(packed)
    raw_own, keys_own, query_own, w_query, w_key, w_mixed = call(
        own_rows_kernel,
        [
            shaped((tokens // 2, width), BF),
            shaped((tokens, width), BF),
            shaped((tokens // 2, width), BF),
            shaped((width, width), BF),
            shaped((width, width), BF),
            shaped((width, width), BF),
        ],
        [gain, packed, own_other, w_query, w_key, w_value, w_out],
        flops=1000,
    )
    raw_own, cache = lax.optimization_barrier((raw_own, cache))
    cached, inner, outer = call(
        functools.partial(cache_kernel, cells),
        [shaped((3, tokens, half), F32)] + [shaped((cells * 3 // 2, LANES), BF)] * 2,
        [cache, weights],
    )
    ahead, cached = lax.optimization_barrier((ahead, cached))
    ahead_other = between_cores(ahead)
    behind, ahead_other = lax.optimization_barrier((behind, ahead_other))
    tiles = [behind, between_cores(behind), ahead, ahead_other]
    up, down = behind, ahead
    groups = []
    for step in range(2, places // 2 + 1):
        down = cycle(down, "space", -1)
        if 2 * step < places:
            up = cycle(up, "space", 1)
            groups.append([up, down])
        else:
            groups.append([down])

    state = [
        shaped((count, LANES), F32),
        shaped((count, LANES), F32),
        shaped((count, width), F32),
    ]
    query, raw, top, total, accum = call(
        first_kernel,
        [shaped((count, width), BF), shaped((count, width), BF)] + state,
        [gain, raw_own, keys_own, query_own, w_query, w_key] + tiles,
        [pltpu.VMEM((3 * tokens, width), BF)],
    )
    for group in groups[:-1]:
        tiles = []
        for tile in group:
            tiles += [tile, cycle(tile, "chan", 1)]
        top, total, accum = call(
            functools.partial(middle_kernel, len(group)),
            state,
            [gain, query, top, total, accum] + tiles,
                )
    tile, accum = lax.optimization_barrier((groups[-1][0], accum))
    tile_other = cycle(tile, "chan", 1)
    act, joined = call(
        last_kernel,
        [shaped((count, width), BF)] * 2,
        [gain, gain_act, w_mixed, query, raw, top, total, accum, tile, tile_other],
        [pltpu.VMEM((count, 1), F32), pltpu.VMEM((count, width), F32)],
    )
    other = cycle(act, "chan", 1)
    received = []
    for back in range(1, min(moments, 3)):
        (term,) = call(
            functools.partial(send_kernel, cells, back),
            [shaped((tokens * 3 // 2, LANES), BF)],
            [act, other, weights],
            )
        received.append(term)
    act, joined, received = lax.optimization_barrier((act, joined, received))
    received = [cycle(term, "tm", 1 + i) for i, term in enumerate(received)]
    keep, give = call(residual_kernel, [shaped((tokens // 2, half), BF)] * 2, [joined])
    theirs = cycle(give, "chan", 1)
    (rest,) = call(
        functools.partial(rest_kernel, cells),
        [shaped((tokens, half), F32)],
        [act, other, cached, keep, theirs, weights],
    )
    inner, outer, act = lax.optimization_barrier((inner, outer, act))
    outer = lax.ppermute(
        outer, "space", [(i, min(max(((i + 1) ^ 1) - 1, 0), places - 1)) for i in range(places)]
    )
    inner = lax.ppermute(inner, "space", [(i, i ^ 1) for i in range(places)])
    (rest,) = call(
        functools.partial(edge_kernel, cells), [shaped((tokens, half), F32)], [rest, outer, inner]
    )
    written = [pltpu.VMEM((tokens, half), BF), pltpu.SemaphoreType.DMA]
    (out,) = call(early_kernel, [shaped((tokens, half), BF)], [rest], written, kept=True)
    (out,) = call(final_kernel, [shaped((tokens, half), BF)], [rest] + received + [out], written, kept=True)
    return out.reshape(1, rows, cells, half)


def solution(mesh):
    return jax.shard_map(
        body,
        mesh=mesh,
        in_specs=(
            P(("clips", "tm"), "space", None, "chan"),
            P("clips", "space", None, None),
            P(),
            P(),
            P(),
            P(),
            P(),
            P(),
            P(None, None, None, None, "chan"),
        ),
        out_specs=P(("clips", "tm"), "space", None, "chan"),
        check_vma=False,
    )
```

```python
import functools
import math
import jax
import jax.numpy as jnp
from jax import lax
from jax.experimental import pallas as pl
from jax.experimental.pallas import tpu as pltpu
from jax.sharding import PartitionSpec as P

EPS = 1e-06
LANES = 128
BF = jnp.bfloat16
F32 = jnp.float32


def cycle(array, axis, by):
    count = lax.axis_size(axis)
    return lax.ppermute(array, axis, [(i, (i + by) % count) for i in range(count)])


def between_cores(array, pieces=2):
    return jnp.concatenate([cycle(piece, "chan", 1) for piece in jnp.split(array, pieces)])


def call(kernel, outs, args, scratch=(), flops=1000, kept=False):
    vmem = pl.BlockSpec(memory_space=pltpu.VMEM)
    anywhere = pl.BlockSpec(memory_space=pl.ANY)
    into = kept and args[-1].shape == outs[0].shape and args[-1].dtype == outs[0].dtype
    return pl.pallas_call(
        kernel,
        out_shape=outs,
        in_specs=[vmem] * (len(args) - into) + [anywhere] * into,
        out_specs=[anywhere if kept else vmem] * len(outs),
        input_output_aliases={len(args) - 1: 0} if into else {},
        scratch_shapes=list(scratch),
        compiler_params=pltpu.CompilerParams(vmem_limit_bytes=36 * 2**20),
        cost_estimate=pl.CostEstimate(flops=flops, bytes_accessed=1000, transcendentals=0),
    )(*args)


def place_of():
    return lax.axis_index("chan"), lax.axis_index("space"), lax.axis_size("space"), lax.axis_index("tm")


def shaped(shape, dtype):
    return jax.ShapeDtypeStruct(shape, dtype)


def dot(a, b):
    return jnp.dot(a, b, preferred_element_type=F32)


def dot_t(a, b):
    return lax.dot_general(a, b, (((1,), (1,)), ((), ())), preferred_element_type=F32)


def pack(x, out):
    tokens = x.shape[0]
    out[:tokens, :] = x[:, :LANES].astype(BF)
    rest = x[:, LANES:]
    out[tokens:, :] = jnp.concatenate([rest[: tokens // 2], rest[tokens // 2 :]], axis=1).astype(BF)


def unpacked(packed):
    tokens = packed.shape[0] * 2 // 3
    rest = packed[tokens:].astype(F32)
    rest = jnp.concatenate([rest[:, : LANES // 2], rest[:, LANES // 2 :]], axis=0)
    return jnp.concatenate([packed[:tokens].astype(F32), rest], axis=1)


def pack_kernel(x, out):
    pack(x[...], out)


def joined_halves(core, mine, theirs):
    a, b = mine[...].astype(F32), theirs[...].astype(F32)
    first = jnp.where(core == 0, a, b)
    second = jnp.where(core == 0, b, a)
    tokens = a.shape[0] * 2 // 3
    turn = lambda v: pltpu.roll(v, LANES // 2, 1)
    low = lax.broadcasted_iota(jnp.int32, (tokens, LANES), 1) < LANES // 2
    middle = turn(second[:tokens])
    left = jnp.concatenate([first[tokens:], turn(first[tokens:])], axis=0)
    right = jnp.concatenate([turn(second[tokens:]), second[tokens:]], axis=0)
    return jnp.concatenate(
        [first[:tokens], jnp.where(low, left, middle), jnp.where(low, middle, right)], axis=1
    )


def rms_scaled(wide, gain):
    factor = lax.rsqrt(jnp.mean(wide * wide, axis=-1, keepdims=True) + EPS)
    return wide * factor * gain.astype(F32)


def attend(query, keys, top, total, accum):
    scores = [dot_t(query, k) for k in keys]
    new_top = top
    for s in scores:
        most = jnp.max(s, axis=-1, keepdims=True)
        new_top = most if new_top is None else jnp.maximum(new_top, most)
    if top is not None:
        fade = jnp.exp2(top - new_top)
        total, accum = total * fade, accum * fade
    for s, k in zip(scores, keys):
        weights = jnp.exp2(s - new_top)
        part = jnp.sum(weights, axis=-1, keepdims=True)
        mixed = dot(weights.astype(BF), k)
        total = part if total is None else total + part
        accum = mixed if accum is None else accum + mixed
    return new_top, total, accum


def queries(rows, w_query, w_key):
    scale = rows.shape[1] ** (-0.5) * math.log2(math.e)
    return (dot_t(dot(rows, w_query).astype(BF), w_key) * scale).astype(BF)


def own_rows_kernel(gain, mine, theirs, w_query, w_key, w_value, w_out, *refs):
    raw_out, keys_out, query_out, w_query_out, w_key_out, w_mixed_out = refs
    core = place_of()[0]
    raw = joined_halves(core, mine, theirs)
    half = raw.shape[0] // 2
    keys = rms_scaled(raw, gain[...]).astype(BF)
    keys_out[...] = keys
    raw_out[...] = jnp.where(core == 0, raw[:half], raw[half:]).astype(BF)
    rows = jnp.where(core == 0, keys[:half], keys[half:])
    query_out[...] = queries(rows, w_query[...], w_key[...])
    w_query_out[...] = w_query[...]
    w_key_out[...] = w_key[...]
    w_mixed_out[...] = dot(w_value[...], w_out[...]).astype(BF)


def first_kernel(gain, raw_own, keys_own, query_own, w_query, w_key, *refs):
    core = place_of()[0]
    tiles, (query_out, raw_out, top_out, total_out, accum_out, keys) = refs[:4], refs[4:]
    tokens = keys_own.shape[0]
    half = tokens // 2
    edge = raw_out.shape[0] - half
    behind, ahead = [joined_halves(core, tiles[2 * i], tiles[2 * i + 1]) for i in range(2)]
    keys[:tokens] = keys_own[...]
    keys[tokens : 2 * tokens] = rms_scaled(behind, gain[...]).astype(BF)
    keys[2 * tokens :] = rms_scaled(ahead, gain[...]).astype(BF)
    beyond = jnp.where(core == 0, behind[tokens - edge :], ahead[:edge])
    rows = jnp.where(core == 0, keys[2 * tokens - edge : 2 * tokens], keys[2 * tokens : 2 * tokens + edge])
    beyond = beyond.astype(BF)
    further = queries(rows, w_query[...], w_key[...])

    def ordered(own, other):
        return jnp.where(
            core == 0, jnp.concatenate([other, own], axis=0), jnp.concatenate([own, other], axis=0)
        )

    raw_out[...] = ordered(raw_own[...], beyond)
    query = ordered(query_own[...], further)
    query_out[...] = query
    top, total, accum = attend(query, [keys[...]], None, None, None)
    top_out[...] = jnp.broadcast_to(top, top_out.shape)
    total_out[...] = jnp.broadcast_to(total, total_out.shape)
    accum_out[...] = accum


def middle_kernel(count, gain, query, top, total, accum, *refs):
    core = place_of()[0]
    tiles, (top_out, total_out, accum_out) = refs[: 2 * count], refs[2 * count :]
    keys = [
        rms_scaled(joined_halves(core, tiles[2 * i], tiles[2 * i + 1]), gain[...]).astype(BF)
        for i in range(count)
    ]
    new = attend(query[...], keys, top[:, :1], total[:, :1], accum[...])
    top_out[...] = jnp.broadcast_to(new[0], top_out.shape)
    total_out[...] = jnp.broadcast_to(new[1], total_out.shape)
    accum_out[...] = new[2]


def last_kernel(gain, gain_two, w_mixed, query, raw, top, total, accum, mine, theirs, *refs):
    core, place, places, _ = place_of()
    act_out, joined_out, total_now, accum_now = refs
    keys = rms_scaled(joined_halves(core, mine, theirs), gain[...]).astype(BF)
    scores = dot_t(query[...], keys)
    weights = jnp.exp2(scores - top[:, :1])
    total_now[...] = total[:, :1] + jnp.sum(weights, axis=-1, keepdims=True)
    accum_now[...] = accum[...] + dot(weights.astype(BF), keys)

    @pl.when(jnp.max(jnp.max(scores, axis=-1, keepdims=True) - top[:, :1]) > 60.0)
    def _():
        _, total_now[...], accum_now[...] = attend(query[...], [keys], top[:, :1], total[:, :1], accum[...])

    mixed = (accum_now[...] * (1.0 / total_now[...])).astype(BF)
    joined = (raw[...].astype(F32) + dot(mixed, w_mixed[...])).astype(BF)
    joined_out[...] = joined
    edge = joined.shape[0] // 3
    act = rms_scaled(joined.astype(F32), gain_two[...])
    act = 0.5 * act
    act = act + act * jnp.tanh(act)
    row = lax.broadcasted_iota(jnp.int32, (act.shape[0], 1), 0)
    beyond = ((core == 0) & (place == 0) & (row < edge)) | (
        (core == 1) & (place == places - 1) & (row >= 2 * edge)
    )
    act_out[...] = jnp.where(beyond, 0.0, act).astype(BF)


def residual_kernel(joined, keep_out, give_out):
    core = place_of()[0]
    edge = joined.shape[0] // 3
    own = jnp.where(core == 0, joined[edge:], joined[: 2 * edge]).astype(F32)
    half = own.shape[1] // 2
    low, high = own[:, :half], own[:, half:]
    keep_out[...] = jnp.where(core == 0, low, high).astype(BF)
    give_out[...] = jnp.where(core == 0, high, low).astype(BF)


def taps(padded, weights, cells):
    tokens = padded.shape[0] - 2 * cells
    wide = jnp.concatenate([padded[i * cells : i * cells + tokens] for i in range(3)], axis=1)
    return [
        dot_t(wide, jnp.concatenate([weights[row, cell] for row in range(3)], axis=1))
        for cell in range(3)
    ]


def gathered(parts, cells):
    left, middle, right = parts
    tokens = middle.shape[0]
    cell = lax.rem(lax.broadcasted_iota(jnp.int32, (tokens, 1), 0), cells)
    left = jnp.where(cell == 0, 0.0, pltpu.roll(left, 1, 0))
    right = jnp.where(cell == cells - 1, 0.0, pltpu.roll(right, tokens - 1, 0))
    return middle + left + right


def by_core(mine, theirs):
    core, a, b = place_of()[0], mine[...], theirs[...]
    return jnp.concatenate([jnp.where(core == 0, a, b), jnp.where(core == 0, b, a)], axis=0)


def send_kernel(cells, back, act, other, weights, out):
    wanted = place_of()[3] + back < lax.axis_size("tm")

    @pl.when(wanted)
    def _():
        pack(gathered(taps(by_core(act, other), weights.at[2 - back], cells), cells), out)

    @pl.when(jnp.logical_not(wanted))
    def _():
        out[...] = jnp.zeros_like(out)


def cache_kernel(cells, cache, weights, sums, inner, outer):
    _, place, _, moment = place_of()
    tokens = cache.shape[1]
    ends = jnp.zeros((cells, cache.shape[2]), cache.dtype)

    def products(pairs):
        for i in range(3):
            sums[i] = sum(
                dot_t(
                    jnp.concatenate([padded[r * cells : r * cells + tokens] for r in range(3)], axis=1),
                    jnp.concatenate([weights[back, row, i] for row in range(3)], axis=1),
                )
                for padded, back in [
                    (jnp.concatenate([ends, cache[frame], ends], axis=0), back) for frame, back in pairs
                ]
            )
        finished = []
        for start, row in ((tokens - cells, 0), (0, 2)):
            edge = jnp.concatenate([cache[frame, start : start + cells] for frame, _ in pairs], axis=1)
            parts = [
                dot_t(edge, jnp.concatenate([weights[back, row, i] for _, back in pairs], axis=1))
                for i in range(3)
            ]
            finished.append(gathered(parts, cells))
        up, down = finished
        even = lax.rem(place, 2) == 0
        pack(jnp.where(even, up, down), inner)
        pack(jnp.where(even, down, up), outer)

    @pl.when(moment == 0)
    def _():
        products([(0, 0), (1, 1)])

    @pl.when(moment == 1)
    def _():
        products([(1, 0)])

    @pl.when(moment > 1)
    def _():
        for out in (sums, inner, outer):
            out[...] = jnp.zeros_like(out)


def rest_kernel(cells, act, other, cached, keep, theirs, weights, out):
    parts = taps(by_core(act, other), weights.at[2], cells)
    terms = gathered([part + cached[i] for i, part in enumerate(parts)], cells)
    out[...] = by_core(keep, theirs).astype(F32) + terms


def edge_kernel(cells, rest, outer, inner, out):
    _, place, places, _ = place_of()
    tokens = rest.shape[0]
    even = lax.rem(place, 2) == 0
    above, below = jnp.where(even, outer[...], inner[...]), jnp.where(even, inner[...], outer[...])
    out[:cells] = rest[:cells] + jnp.where(place == 0, 0.0, unpacked(above))
    out[cells : tokens - cells] = rest[cells : tokens - cells]
    out[tokens - cells :] = rest[tokens - cells :] + jnp.where(place == places - 1, 0.0, unpacked(below))


def write(total, out, held, sem):
    held[...] = total.astype(BF)
    copy = pltpu.make_async_copy(held, out, sem)
    copy.start()
    copy.wait()


def early_kernel(rest, out, held, sem):
    @pl.when(place_of()[3] == 0)
    def _():
        write(rest[...], out, held, sem)


def final_kernel(rest, *refs):
    moment = place_of()[3]
    received, (_, out, held, sem) = refs[:-4], refs[-4:]

    @pl.when(moment > 0)
    def _():
        total = rest[...]
        for back, ref in enumerate(received):
            total = total + jnp.where(moment > back, unpacked(ref[...]), 0.0)
        write(total, out, held, sem)


def body(frames_in, cache, gain_one, gain_two, w_query, w_key, w_value, w_out, conv_weight):
    places, moments = lax.axis_size("space"), lax.axis_size("tm")
    _, rows, cells, half = frames_in.shape
    tokens, width = rows * cells, 2 * half
    count = tokens // 2 + cells

    gain = gain_one.reshape(1, width)
    gain_act = gain_two.reshape(1, width)
    weights = conv_weight.transpose(0, 1, 2, 4, 3)

    (packed,) = call(
        pack_kernel,
        [shaped((tokens * 3 // 2, LANES), BF)],
        [frames_in.reshape(tokens, half)],
        flops=4 * 10**9,
    )
    behind, ahead = cycle(packed, "space", 1), cycle(packed, "space", -1)
    cache = cache.reshape(2, tokens, width)
    own_other = between_cores(packed)
    raw_own, keys_own, query_own, w_query, w_key, w_mixed = call(
        own_rows_kernel,
        [
            shaped((tokens // 2, width), BF),
            shaped((tokens, width), BF),
            shaped((tokens // 2, width), BF),
            shaped((width, width), BF),
            shaped((width, width), BF),
            shaped((width, width), BF),
        ],
        [gain, packed, own_other, w_query, w_key, w_value, w_out],
        flops=1000,
    )
    raw_own, cache = lax.optimization_barrier((raw_own, cache))
    cached, inner, outer = call(
        functools.partial(cache_kernel, cells),
        [shaped((3, tokens, half), F32)] + [shaped((cells * 3 // 2, LANES), BF)] * 2,
        [cache, weights],
    )
    ahead, cached = lax.optimization_barrier((ahead, cached))
    ahead_other = between_cores(ahead)
    behind, ahead_other = lax.optimization_barrier((behind, ahead_other))
    tiles = [behind, between_cores(behind), ahead, ahead_other]
    up, down = behind, ahead
    groups = []
    for step in range(2, places // 2 + 1):
        down = cycle(down, "space", -1)
        if 2 * step < places:
            up = cycle(up, "space", 1)
            groups.append([up, down])
        else:
            groups.append([down])

    state = [
        shaped((count, LANES), F32),
        shaped((count, LANES), F32),
        shaped((count, width), F32),
    ]
    query, raw, top, total, accum = call(
        first_kernel,
        [shaped((count, width), BF), shaped((count, width), BF)] + state,
        [gain, raw_own, keys_own, query_own, w_query, w_key] + tiles,
        [pltpu.VMEM((3 * tokens, width), BF)],
    )
    for group in groups[:-1]:
        tiles = []
        for tile in group:
            tiles += [tile, cycle(tile, "chan", 1)]
        top, total, accum = call(
            functools.partial(middle_kernel, len(group)),
            state,
            [gain, query, top, total, accum] + tiles,
                )
    tile, accum = lax.optimization_barrier((groups[-1][0], accum))
    tile_other = cycle(tile, "chan", 1)
    act, joined = call(
        last_kernel,
        [shaped((count, width), BF)] * 2,
        [gain, gain_act, w_mixed, query, raw, top, total, accum, tile, tile_other],
        [pltpu.VMEM((count, 1), F32), pltpu.VMEM((count, width), F32)],
    )
    other = cycle(act, "chan", 1)
    received = []
    for back in range(1, min(moments, 3)):
        (term,) = call(
            functools.partial(send_kernel, cells, back),
            [shaped((tokens * 3 // 2, LANES), BF)],
            [act, other, weights],
            )
        received.append(term)
    act, joined, received = lax.optimization_barrier((act, joined, received))
    received = [cycle(term, "tm", 1 + i) for i, term in enumerate(received)]
    keep, give = call(residual_kernel, [shaped((tokens // 2, half), BF)] * 2, [joined])
    theirs = cycle(give, "chan", 1)
    (rest,) = call(
        functools.partial(rest_kernel, cells),
        [shaped((tokens, half), F32)],
        [act, other, cached, keep, theirs, weights],
    )
    inner, outer, act = lax.optimization_barrier((inner, outer, act))
    outer = lax.ppermute(
        outer, "space", [(i, min(max(((i + 1) ^ 1) - 1, 0), places - 1)) for i in range(places)]
    )
    inner = lax.ppermute(inner, "space", [(i, i ^ 1) for i in range(places)])
    (rest,) = call(
        functools.partial(edge_kernel, cells), [shaped((tokens, half), F32)], [rest, outer, inner]
    )
    written = [pltpu.VMEM((tokens, half), BF), pltpu.SemaphoreType.DMA]
    (out,) = call(early_kernel, [shaped((tokens, half), BF)], [rest], written, kept=True)
    (out,) = call(final_kernel, [shaped((tokens, half), BF)], [rest] + received + [out], written, kept=True)
    return out.reshape(1, rows, cells, half)


def solution(mesh):
    return jax.shard_map(
        body,
        mesh=mesh,
        in_specs=(
            P(("clips", "tm"), "space", None, "chan"),
            P("clips", "space", None, None),
            P(),
            P(),
            P(),
            P(),
            P(),
            P(),
            P(None, None, None, None, "chan"),
        ),
        out_specs=P(("clips", "tm"), "space", None, "chan"),
        check_vma=False,
    )
```

```python
import functools
import math
import jax
import jax.numpy as jnp
from jax import lax
from jax.experimental import pallas as pl
from jax.experimental.pallas import tpu as pltpu
from jax.sharding import PartitionSpec as P

EPS = 1e-06
LANES = 128
BF = jnp.bfloat16
F32 = jnp.float32


def cycle(array, axis, by):
    count = lax.axis_size(axis)
    return lax.ppermute(array, axis, [(i, (i + by) % count) for i in range(count)])


def between_cores(array, pieces=2):
    return jnp.concatenate([cycle(piece, "chan", 1) for piece in jnp.split(array, pieces)])


def call(kernel, outs, args, scratch=(), flops=1000, kept=False):
    vmem = pl.BlockSpec(memory_space=pltpu.VMEM)
    anywhere = pl.BlockSpec(memory_space=pl.ANY)
    into = kept and args[-1].shape == outs[0].shape and args[-1].dtype == outs[0].dtype
    return pl.pallas_call(
        kernel,
        out_shape=outs,
        in_specs=[vmem] * (len(args) - into) + [anywhere] * into,
        out_specs=[anywhere if kept else vmem] * len(outs),
        input_output_aliases={len(args) - 1: 0} if into else {},
        scratch_shapes=list(scratch),
        compiler_params=pltpu.CompilerParams(vmem_limit_bytes=36 * 2**20),
        cost_estimate=pl.CostEstimate(flops=flops, bytes_accessed=1000, transcendentals=0),
    )(*args)


def place_of():
    return lax.axis_index("chan"), lax.axis_index("space"), lax.axis_size("space"), lax.axis_index("tm")


def shaped(shape, dtype):
    return jax.ShapeDtypeStruct(shape, dtype)


def dot(a, b):
    return jnp.dot(a, b, preferred_element_type=F32)


def dot_t(a, b):
    return lax.dot_general(a, b, (((1,), (1,)), ((), ())), preferred_element_type=F32)


def pack(x, out):
    tokens = x.shape[0]
    out[:tokens, :] = x[:, :LANES].astype(BF)
    rest = x[:, LANES:]
    out[tokens:, :] = jnp.concatenate([rest[: tokens // 2], rest[tokens // 2 :]], axis=1).astype(BF)


def unpacked(packed):
    tokens = packed.shape[0] * 2 // 3
    rest = packed[tokens:].astype(F32)
    rest = jnp.concatenate([rest[:, : LANES // 2], rest[:, LANES // 2 :]], axis=0)
    return jnp.concatenate([packed[:tokens].astype(F32), rest], axis=1)


def pack_kernel(x, out):
    pack(x[...], out)


def joined_halves(core, mine, theirs):
    a, b = mine[...].astype(F32), theirs[...].astype(F32)
    first = jnp.where(core == 0, a, b)
    second = jnp.where(core == 0, b, a)
    tokens = a.shape[0] * 2 // 3
    turn = lambda v: pltpu.roll(v, LANES // 2, 1)
    low = lax.broadcasted_iota(jnp.int32, (tokens, LANES), 1) < LANES // 2
    middle = turn(second[:tokens])
    left = jnp.concatenate([first[tokens:], turn(first[tokens:])], axis=0)
    right = jnp.concatenate([turn(second[tokens:]), second[tokens:]], axis=0)
    return jnp.concatenate(
        [first[:tokens], jnp.where(low, left, middle), jnp.where(low, middle, right)], axis=1
    )


def rms_scaled(wide, gain):
    factor = lax.rsqrt(jnp.mean(wide * wide, axis=-1, keepdims=True) + EPS)
    return wide * factor * gain.astype(F32)


def attend(query, keys, top, total, accum):
    scores = [dot_t(query, k) for k in keys]
    new_top = top
    for s in scores:
        most = jnp.max(s, axis=-1, keepdims=True)
        new_top = most if new_top is None else jnp.maximum(new_top, most)
    if top is not None:
        fade = jnp.exp2(top - new_top)
        total, accum = total * fade, accum * fade
    for s, k in zip(scores, keys):
        weights = jnp.exp2(s - new_top)
        part = jnp.sum(weights, axis=-1, keepdims=True)
        mixed = dot(weights.astype(BF), k)
        total = part if total is None else total + part
        accum = mixed if accum is None else accum + mixed
    return new_top, total, accum


def queries(rows, w_query, w_key):
    scale = rows.shape[1] ** (-0.5) * math.log2(math.e)
    return (dot_t(dot(rows, w_query).astype(BF), w_key) * scale).astype(BF)


def own_rows_kernel(gain, mine, theirs, w_query, w_key, w_value, w_out, *refs):
    raw_out, keys_out, query_out, w_query_out, w_key_out, w_mixed_out = refs
    core = place_of()[0]
    raw = joined_halves(core, mine, theirs)
    half = raw.shape[0] // 2
    keys = rms_scaled(raw, gain[...]).astype(BF)
    keys_out[...] = keys
    raw_out[...] = jnp.where(core == 0, raw[:half], raw[half:]).astype(BF)
    rows = jnp.where(core == 0, keys[:half], keys[half:])
    query_out[...] = queries(rows, w_query[...], w_key[...])
    w_query_out[...] = w_query[...]
    w_key_out[...] = w_key[...]
    w_mixed_out[...] = dot(w_value[...], w_out[...]).astype(BF)


def first_kernel(gain, raw_own, keys_own, query_own, w_query, w_key, *refs):
    core = place_of()[0]
    tiles, (query_out, raw_out, top_out, total_out, accum_out, keys) = refs[:4], refs[4:]
    tokens = keys_own.shape[0]
    half = tokens // 2
    edge = raw_out.shape[0] - half
    behind, ahead = [joined_halves(core, tiles[2 * i], tiles[2 * i + 1]) for i in range(2)]
    keys[:tokens] = keys_own[...]
    keys[tokens : 2 * tokens] = rms_scaled(behind, gain[...]).astype(BF)
    keys[2 * tokens :] = rms_scaled(ahead, gain[...]).astype(BF)
    beyond = jnp.where(core == 0, behind[tokens - edge :], ahead[:edge])
    rows = jnp.where(core == 0, keys[2 * tokens - edge : 2 * tokens], keys[2 * tokens : 2 * tokens + edge])
    beyond = beyond.astype(BF)
    further = queries(rows, w_query[...], w_key[...])

    def ordered(own, other):
        return jnp.where(
            core == 0, jnp.concatenate([other, own], axis=0), jnp.concatenate([own, other], axis=0)
        )

    raw_out[...] = ordered(raw_own[...], beyond)
    query = ordered(query_own[...], further)
    query_out[...] = query
    top, total, accum = attend(query, [keys[...]], None, None, None)
    top_out[...] = jnp.broadcast_to(top, top_out.shape)
    total_out[...] = jnp.broadcast_to(total, total_out.shape)
    accum_out[...] = accum


def middle_kernel(count, gain, query, top, total, accum, *refs):
    core = place_of()[0]
    tiles, (top_out, total_out, accum_out) = refs[: 2 * count], refs[2 * count :]
    keys = [
        rms_scaled(joined_halves(core, tiles[2 * i], tiles[2 * i + 1]), gain[...]).astype(BF)
        for i in range(count)
    ]
    new = attend(query[...], keys, top[:, :1], total[:, :1], accum[...])
    top_out[...] = jnp.broadcast_to(new[0], top_out.shape)
    total_out[...] = jnp.broadcast_to(new[1], total_out.shape)
    accum_out[...] = new[2]


def last_kernel(gain, gain_two, w_mixed, query, raw, top, total, accum, mine, theirs, *refs):
    core, place, places, _ = place_of()
    act_out, joined_out, total_now, accum_now = refs
    keys = rms_scaled(joined_halves(core, mine, theirs), gain[...]).astype(BF)
    scores = dot_t(query[...], keys)
    weights = jnp.exp2(scores - top[:, :1])
    total_now[...] = total[:, :1] + jnp.sum(weights, axis=-1, keepdims=True)
    accum_now[...] = accum[...] + dot(weights.astype(BF), keys)

    @pl.when(jnp.max(jnp.max(scores, axis=-1, keepdims=True) - top[:, :1]) > 60.0)
    def _():
        _, total_now[...], accum_now[...] = attend(query[...], [keys], top[:, :1], total[:, :1], accum[...])

    mixed = (accum_now[...] * (1.0 / total_now[...])).astype(BF)
    joined = (raw[...].astype(F32) + dot(mixed, w_mixed[...])).astype(BF)
    joined_out[...] = joined
    edge = joined.shape[0] // 3
    act = rms_scaled(joined.astype(F32), gain_two[...])
    act = 0.5 * act
    act = act + act * jnp.tanh(act)
    row = lax.broadcasted_iota(jnp.int32, (act.shape[0], 1), 0)
    beyond = ((core == 0) & (place == 0) & (row < edge)) | (
        (core == 1) & (place == places - 1) & (row >= 2 * edge)
    )
    act_out[...] = jnp.where(beyond, 0.0, act).astype(BF)


def residual_kernel(joined, keep_out, give_out):
    core = place_of()[0]
    edge = joined.shape[0] // 3
    own = jnp.where(core == 0, joined[edge:], joined[: 2 * edge]).astype(F32)
    half = own.shape[1] // 2
    low, high = own[:, :half], own[:, half:]
    keep_out[...] = jnp.where(core == 0, low, high).astype(BF)
    give_out[...] = jnp.where(core == 0, high, low).astype(BF)


def taps(padded, weights, cells):
    tokens = padded.shape[0] - 2 * cells
    wide = jnp.concatenate([padded[i * cells : i * cells + tokens] for i in range(3)], axis=1)
    return [
        dot_t(wide, jnp.concatenate([weights[row, cell] for row in range(3)], axis=1))
        for cell in range(3)
    ]


def gathered(parts, cells):
    left, middle, right = parts
    tokens = middle.shape[0]
    cell = lax.rem(lax.broadcasted_iota(jnp.int32, (tokens, 1), 0), cells)
    left = jnp.where(cell == 0, 0.0, pltpu.roll(left, 1, 0))
    right = jnp.where(cell == cells - 1, 0.0, pltpu.roll(right, tokens - 1, 0))
    return middle + left + right


def by_core(mine, theirs):
    core, a, b = place_of()[0], mine[...], theirs[...]
    return jnp.concatenate([jnp.where(core == 0, a, b), jnp.where(core == 0, b, a)], axis=0)


def near_kernel(cells, back, act, weights, out):
    @pl.when(place_of()[3] + back < lax.axis_size("tm"))
    def _():
        out[...] = gathered(taps(act, weights.at[2 - back], cells), cells)


def send_kernel(cells, back, near, act, other, weights, out):
    wanted = place_of()[3] + back < lax.axis_size("tm")

    @pl.when(wanted)
    def _():
        core, mine, theirs = place_of()[0], act[...], other[...]
        own = mine.shape[0] - cells
        padded = jnp.where(
            core == 0,
            jnp.concatenate([mine[cells:], theirs], axis=0),
            jnp.concatenate([theirs, mine[:own]], axis=0),
        )
        rows = gathered(taps(padded, weights.at[2 - back], cells), cells)
        pack(
            jnp.where(
                core == 0,
                jnp.concatenate([near[...], rows], axis=0),
                jnp.concatenate([rows, near[...]], axis=0),
            ),
            out,
        )

    @pl.when(jnp.logical_not(wanted))
    def _():
        out[...] = jnp.zeros_like(out)


def cache_kernel(cells, cache, weights, sums, inner, outer):
    _, place, _, moment = place_of()
    tokens = cache.shape[1]
    ends = jnp.zeros((cells, cache.shape[2]), cache.dtype)

    def products(pairs):
        for i in range(3):
            sums[i] = sum(
                dot_t(
                    jnp.concatenate([padded[r * cells : r * cells + tokens] for r in range(3)], axis=1),
                    jnp.concatenate([weights[back, row, i] for row in range(3)], axis=1),
                )
                for padded, back in [
                    (jnp.concatenate([ends, cache[frame], ends], axis=0), back) for frame, back in pairs
                ]
            )
        finished = []
        for start, row in ((tokens - cells, 0), (0, 2)):
            edge = jnp.concatenate([cache[frame, start : start + cells] for frame, _ in pairs], axis=1)
            parts = [
                dot_t(edge, jnp.concatenate([weights[back, row, i] for _, back in pairs], axis=1))
                for i in range(3)
            ]
            finished.append(gathered(parts, cells))
        up, down = finished
        even = lax.rem(place, 2) == 0
        pack(jnp.where(even, up, down), inner)
        pack(jnp.where(even, down, up), outer)

    @pl.when(moment == 0)
    def _():
        products([(0, 0), (1, 1)])

    @pl.when(moment == 1)
    def _():
        products([(1, 0)])

    @pl.when(moment > 1)
    def _():
        for out in (sums, inner, outer):
            out[...] = jnp.zeros_like(out)


def rest_kernel(cells, act, other, cached, keep, theirs, weights, out):
    parts = taps(by_core(act, other), weights.at[2], cells)
    terms = gathered([part + cached[i] for i, part in enumerate(parts)], cells)
    out[...] = by_core(keep, theirs).astype(F32) + terms


def edge_kernel(cells, rest, outer, inner, out):
    _, place, places, _ = place_of()
    tokens = rest.shape[0]
    even = lax.rem(place, 2) == 0
    above, below = jnp.where(even, outer[...], inner[...]), jnp.where(even, inner[...], outer[...])
    out[:cells] = rest[:cells] + jnp.where(place == 0, 0.0, unpacked(above))
    out[cells : tokens - cells] = rest[cells : tokens - cells]
    out[tokens - cells :] = rest[tokens - cells :] + jnp.where(place == places - 1, 0.0, unpacked(below))


def write(total, out, held, sem):
    held[...] = total.astype(BF)
    copy = pltpu.make_async_copy(held, out, sem)
    copy.start()
    copy.wait()


def early_kernel(rest, out, held, sem):
    @pl.when(place_of()[3] == 0)
    def _():
        write(rest[...], out, held, sem)


def final_kernel(rest, *refs):
    moment = place_of()[3]
    received, (_, out, held, sem) = refs[:-4], refs[-4:]

    @pl.when(moment > 0)
    def _():
        total = rest[...]
        for back, ref in enumerate(received):
            total = total + jnp.where(moment > back, unpacked(ref[...]), 0.0)
        write(total, out, held, sem)


def body(frames_in, cache, gain_one, gain_two, w_query, w_key, w_value, w_out, conv_weight):
    places, moments = lax.axis_size("space"), lax.axis_size("tm")
    _, rows, cells, half = frames_in.shape
    tokens, width = rows * cells, 2 * half
    count = tokens // 2 + cells

    gain = gain_one.reshape(1, width)
    gain_act = gain_two.reshape(1, width)
    weights = conv_weight.transpose(0, 1, 2, 4, 3)

    (packed,) = call(
        pack_kernel,
        [shaped((tokens * 3 // 2, LANES), BF)],
        [frames_in.reshape(tokens, half)],
        flops=4 * 10**9,
    )
    behind, ahead = cycle(packed, "space", 1), cycle(packed, "space", -1)
    cache = cache.reshape(2, tokens, width)
    own_other = between_cores(packed)
    raw_own, keys_own, query_own, w_query, w_key, w_mixed = call(
        own_rows_kernel,
        [
            shaped((tokens // 2, width), BF),
            shaped((tokens, width), BF),
            shaped((tokens // 2, width), BF),
            shaped((width, width), BF),
            shaped((width, width), BF),
            shaped((width, width), BF),
        ],
        [gain, packed, own_other, w_query, w_key, w_value, w_out],
        flops=1000,
    )
    raw_own, cache = lax.optimization_barrier((raw_own, cache))
    cached, inner, outer = call(
        functools.partial(cache_kernel, cells),
        [shaped((3, tokens, half), F32)] + [shaped((cells * 3 // 2, LANES), BF)] * 2,
        [cache, weights],
    )
    ahead, cached = lax.optimization_barrier((ahead, cached))
    ahead_other = between_cores(ahead)
    behind, ahead_other = lax.optimization_barrier((behind, ahead_other))
    tiles = [behind, between_cores(behind), ahead, ahead_other]
    up, down = behind, ahead
    groups = []
    for step in range(2, places // 2 + 1):
        down = cycle(down, "space", -1)
        if 2 * step < places:
            up = cycle(up, "space", 1)
            groups.append([up, down])
        else:
            groups.append([down])

    state = [
        shaped((count, LANES), F32),
        shaped((count, LANES), F32),
        shaped((count, width), F32),
    ]
    query, raw, top, total, accum = call(
        first_kernel,
        [shaped((count, width), BF), shaped((count, width), BF)] + state,
        [gain, raw_own, keys_own, query_own, w_query, w_key] + tiles,
        [pltpu.VMEM((3 * tokens, width), BF)],
    )
    for group in groups[:-1]:
        tiles = []
        for tile in group:
            tiles += [tile, cycle(tile, "chan", 1)]
        top, total, accum = call(
            functools.partial(middle_kernel, len(group)),
            state,
            [gain, query, top, total, accum] + tiles,
                )
    tile, accum = lax.optimization_barrier((groups[-1][0], accum))
    tile_other = cycle(tile, "chan", 1)
    act, joined = call(
        last_kernel,
        [shaped((count, width), BF)] * 2,
        [gain, gain_act, w_mixed, query, raw, top, total, accum, tile, tile_other],
        [pltpu.VMEM((count, 1), F32), pltpu.VMEM((count, width), F32)],
    )
    other = cycle(act, "chan", 1)
    received = []
    for back in range(1, min(moments, 3)):
        (near,) = call(
            functools.partial(near_kernel, cells, back), [shaped((cells, half), F32)], [act, weights]
        )
        (term,) = call(
            functools.partial(send_kernel, cells, back),
            [shaped((tokens * 3 // 2, LANES), BF)],
            [near, act, other, weights],
            )
        received.append(term)
    act, joined, received = lax.optimization_barrier((act, joined, received))
    received = [cycle(term, "tm", 1 + i) for i, term in enumerate(received)]
    keep, give = call(residual_kernel, [shaped((tokens // 2, half), BF)] * 2, [joined])
    theirs = cycle(give, "chan", 1)
    (rest,) = call(
        functools.partial(rest_kernel, cells),
        [shaped((tokens, half), F32)],
        [act, other, cached, keep, theirs, weights],
    )
    inner, outer, act = lax.optimization_barrier((inner, outer, act))
    outer = lax.ppermute(
        outer, "space", [(i, min(max(((i + 1) ^ 1) - 1, 0), places - 1)) for i in range(places)]
    )
    inner = lax.ppermute(inner, "space", [(i, i ^ 1) for i in range(places)])
    (rest,) = call(
        functools.partial(edge_kernel, cells), [shaped((tokens, half), F32)], [rest, outer, inner]
    )
    written = [pltpu.VMEM((tokens, half), BF), pltpu.SemaphoreType.DMA]
    (out,) = call(early_kernel, [shaped((tokens, half), BF)], [rest], written, kept=True)
    (out,) = call(final_kernel, [shaped((tokens, half), BF)], [rest] + received + [out], written, kept=True)
    return out.reshape(1, rows, cells, half)


def solution(mesh):
    return jax.shard_map(
        body,
        mesh=mesh,
        in_specs=(
            P(("clips", "tm"), "space", None, "chan"),
            P("clips", "space", None, None),
            P(),
            P(),
            P(),
            P(),
            P(),
            P(),
            P(None, None, None, None, "chan"),
        ),
        out_specs=P(("clips", "tm"), "space", None, "chan"),
        check_vma=False,
    )
```

```python
import functools
import math
import jax
import jax.numpy as jnp
from jax import lax
from jax.experimental import pallas as pl
from jax.experimental.pallas import tpu as pltpu
from jax.sharding import PartitionSpec as P

EPS = 1e-06
LANES = 128
BF = jnp.bfloat16
F32 = jnp.float32


def cycle(array, axis, by):
    count = lax.axis_size(axis)
    return lax.ppermute(array, axis, [(i, (i + by) % count) for i in range(count)])


def between_cores(array, pieces=2):
    return jnp.concatenate([cycle(piece, "chan", 1) for piece in jnp.split(array, pieces)])


def call(kernel, outs, args, scratch=(), flops=1000, kept=False):
    vmem = pl.BlockSpec(memory_space=pltpu.VMEM)
    anywhere = pl.BlockSpec(memory_space=pl.ANY)
    into = kept and args[-1].shape == outs[0].shape and args[-1].dtype == outs[0].dtype
    return pl.pallas_call(
        kernel,
        out_shape=outs,
        in_specs=[vmem] * (len(args) - into) + [anywhere] * into,
        out_specs=[anywhere if kept else vmem] * len(outs),
        input_output_aliases={len(args) - 1: 0} if into else {},
        scratch_shapes=list(scratch),
        compiler_params=pltpu.CompilerParams(vmem_limit_bytes=36 * 2**20),
        cost_estimate=pl.CostEstimate(flops=flops, bytes_accessed=1000, transcendentals=0),
    )(*args)


def place_of():
    return lax.axis_index("chan"), lax.axis_index("space"), lax.axis_size("space"), lax.axis_index("tm")


def shaped(shape, dtype):
    return jax.ShapeDtypeStruct(shape, dtype)


def dot(a, b):
    return jnp.dot(a, b, preferred_element_type=F32)


def dot_t(a, b):
    return lax.dot_general(a, b, (((1,), (1,)), ((), ())), preferred_element_type=F32)


def pack(x, out):
    tokens = x.shape[0]
    out[:tokens, :] = x[:, :LANES].astype(BF)
    rest = x[:, LANES:]
    out[tokens:, :] = jnp.concatenate([rest[: tokens // 2], rest[tokens // 2 :]], axis=1).astype(BF)


def unpacked(packed):
    tokens = packed.shape[0] * 2 // 3
    rest = packed[tokens:].astype(F32)
    rest = jnp.concatenate([rest[:, : LANES // 2], rest[:, LANES // 2 :]], axis=0)
    return jnp.concatenate([packed[:tokens].astype(F32), rest], axis=1)


def pack_kernel(x, out):
    pack(x[...], out)


def joined_halves(core, mine, theirs):
    a, b = mine[...].astype(F32), theirs[...].astype(F32)
    first = jnp.where(core == 0, a, b)
    second = jnp.where(core == 0, b, a)
    tokens = a.shape[0] * 2 // 3
    turn = lambda v: pltpu.roll(v, LANES // 2, 1)
    low = lax.broadcasted_iota(jnp.int32, (tokens, LANES), 1) < LANES // 2
    middle = turn(second[:tokens])
    left = jnp.concatenate([first[tokens:], turn(first[tokens:])], axis=0)
    right = jnp.concatenate([turn(second[tokens:]), second[tokens:]], axis=0)
    return jnp.concatenate(
        [first[:tokens], jnp.where(low, left, middle), jnp.where(low, middle, right)], axis=1
    )


def rms_scaled(wide, gain):
    factor = lax.rsqrt(jnp.mean(wide * wide, axis=-1, keepdims=True) + EPS)
    return wide * factor * gain.astype(F32)


def attend(query, keys, top, total, accum):
    scores = [dot_t(query, k) for k in keys]
    new_top = top
    for s in scores:
        most = jnp.max(s, axis=-1, keepdims=True)
        new_top = most if new_top is None else jnp.maximum(new_top, most)
    if top is not None:
        fade = jnp.exp2(top - new_top)
        total, accum = total * fade, accum * fade
    for s, k in zip(scores, keys):
        weights = jnp.exp2(s - new_top)
        part = jnp.sum(weights, axis=-1, keepdims=True)
        mixed = dot(weights.astype(BF), k)
        total = part if total is None else total + part
        accum = mixed if accum is None else accum + mixed
    return new_top, total, accum


def queries(rows, w_query, w_key):
    scale = rows.shape[1] ** (-0.5) * math.log2(math.e)
    return (dot_t(dot(rows, w_query).astype(BF), w_key) * scale).astype(BF)


def own_rows_kernel(gain, mine, theirs, w_query, w_key, w_value, w_out, *refs):
    raw_out, keys_out, query_out, w_query_out, w_key_out, w_mixed_out = refs
    core = place_of()[0]
    raw = joined_halves(core, mine, theirs)
    half = raw.shape[0] // 2
    keys = rms_scaled(raw, gain[...]).astype(BF)
    keys_out[...] = keys
    raw_out[...] = jnp.where(core == 0, raw[:half], raw[half:]).astype(BF)
    rows = jnp.where(core == 0, keys[:half], keys[half:])
    query_out[...] = queries(rows, w_query[...], w_key[...])
    w_query_out[...] = w_query[...]
    w_key_out[...] = w_key[...]
    w_mixed_out[...] = dot(w_value[...], w_out[...]).astype(BF)


def first_kernel(gain, raw_own, keys_own, query_own, w_query, w_key, *refs):
    core = place_of()[0]
    tiles, (query_out, raw_out, top_out, total_out, accum_out, keys) = refs[:4], refs[4:]
    tokens = keys_own.shape[0]
    half = tokens // 2
    edge = raw_out.shape[0] - half
    behind, ahead = [joined_halves(core, tiles[2 * i], tiles[2 * i + 1]) for i in range(2)]
    keys[:tokens] = keys_own[...]
    keys[tokens : 2 * tokens] = rms_scaled(behind, gain[...]).astype(BF)
    keys[2 * tokens :] = rms_scaled(ahead, gain[...]).astype(BF)
    beyond = jnp.where(core == 0, behind[tokens - edge :], ahead[:edge])
    rows = jnp.where(core == 0, keys[2 * tokens - edge : 2 * tokens], keys[2 * tokens : 2 * tokens + edge])
    beyond = beyond.astype(BF)
    further = queries(rows, w_query[...], w_key[...])

    def ordered(own, other):
        return jnp.where(
            core == 0, jnp.concatenate([other, own], axis=0), jnp.concatenate([own, other], axis=0)
        )

    raw_out[...] = ordered(raw_own[...], beyond)
    query = ordered(query_own[...], further)
    query_out[...] = query
    top, total, accum = attend(query, [keys[...]], None, None, None)
    top_out[...] = jnp.broadcast_to(top, top_out.shape)
    total_out[...] = jnp.broadcast_to(total, total_out.shape)
    accum_out[...] = accum


def middle_kernel(count, gain, query, top, total, accum, *refs):
    core = place_of()[0]
    tiles, (top_out, total_out, accum_out) = refs[: 2 * count], refs[2 * count :]
    keys = [
        rms_scaled(joined_halves(core, tiles[2 * i], tiles[2 * i + 1]), gain[...]).astype(BF)
        for i in range(count)
    ]
    new = attend(query[...], keys, top[:, :1], total[:, :1], accum[...])
    top_out[...] = jnp.broadcast_to(new[0], top_out.shape)
    total_out[...] = jnp.broadcast_to(new[1], total_out.shape)
    accum_out[...] = new[2]


def last_kernel(gain, gain_two, w_mixed, query, raw, top, total, accum, mine, theirs, *refs):
    core, place, places, _ = place_of()
    act_out, joined_out, total_now, accum_now = refs
    keys = rms_scaled(joined_halves(core, mine, theirs), gain[...]).astype(BF)
    scores = dot_t(query[...], keys)
    weights = jnp.exp2(scores - top[:, :1])
    total_now[...] = total[:, :1] + jnp.sum(weights, axis=-1, keepdims=True)
    accum_now[...] = accum[...] + dot(weights.astype(BF), keys)

    @pl.when(jnp.max(jnp.max(scores, axis=-1, keepdims=True) - top[:, :1]) > 60.0)
    def _():
        _, total_now[...], accum_now[...] = attend(query[...], [keys], top[:, :1], total[:, :1], accum[...])

    mixed = (accum_now[...] * (1.0 / total_now[...])).astype(BF)
    joined = (raw[...].astype(F32) + dot(mixed, w_mixed[...])).astype(BF)
    joined_out[...] = joined
    edge = joined.shape[0] // 3
    act = rms_scaled(joined.astype(F32), gain_two[...])
    act = 0.5 * act
    act = act + act * jnp.tanh(act)
    row = lax.broadcasted_iota(jnp.int32, (act.shape[0], 1), 0)
    beyond = ((core == 0) & (place == 0) & (row < edge)) | (
        (core == 1) & (place == places - 1) & (row >= 2 * edge)
    )
    act_out[...] = jnp.where(beyond, 0.0, act).astype(BF)


def residual_kernel(joined, keep_out, give_out):
    core = place_of()[0]
    edge = joined.shape[0] // 3
    own = jnp.where(core == 0, joined[edge:], joined[: 2 * edge]).astype(F32)
    half = own.shape[1] // 2
    low, high = own[:, :half], own[:, half:]
    keep_out[...] = jnp.where(core == 0, low, high).astype(BF)
    give_out[...] = jnp.where(core == 0, high, low).astype(BF)


def taps(padded, weights, cells):
    tokens = padded.shape[0] - 2 * cells
    wide = jnp.concatenate([padded[i * cells : i * cells + tokens] for i in range(3)], axis=1)
    return [
        dot_t(wide, jnp.concatenate([weights[row, cell] for row in range(3)], axis=1))
        for cell in range(3)
    ]


def gathered(parts, cells):
    left, middle, right = parts
    tokens = middle.shape[0]
    cell = lax.rem(lax.broadcasted_iota(jnp.int32, (tokens, 1), 0), cells)
    left = jnp.where(cell == 0, 0.0, pltpu.roll(left, 1, 0))
    right = jnp.where(cell == cells - 1, 0.0, pltpu.roll(right, tokens - 1, 0))
    return middle + left + right


def by_core(mine, theirs):
    core, a, b = place_of()[0], mine[...], theirs[...]
    return jnp.concatenate([jnp.where(core == 0, a, b), jnp.where(core == 0, b, a)], axis=0)


def near_kernel(cells, back, act, weights, out):
    @pl.when(place_of()[3] + back < lax.axis_size("tm"))
    def _():
        out[...] = gathered(taps(act, weights.at[2 - back], cells), cells)


def send_kernel(cells, back, near, act, other, weights, out):
    wanted = place_of()[3] + back < lax.axis_size("tm")

    @pl.when(wanted)
    def _():
        core, mine, theirs = place_of()[0], act[...], other[...]
        own = mine.shape[0] - cells
        padded = jnp.where(
            core == 0,
            jnp.concatenate([mine[cells:], theirs], axis=0),
            jnp.concatenate([theirs, mine[:own]], axis=0),
        )
        rows = gathered(taps(padded, weights.at[2 - back], cells), cells)
        pack(
            jnp.where(
                core == 0,
                jnp.concatenate([near[...], rows], axis=0),
                jnp.concatenate([rows, near[...]], axis=0),
            ),
            out,
        )

    @pl.when(jnp.logical_not(wanted))
    def _():
        out[...] = jnp.zeros_like(out)


def cache_kernel(cells, cache, weights, sums, inner, outer):
    _, place, _, moment = place_of()
    tokens = cache.shape[1]
    ends = jnp.zeros((cells, cache.shape[2]), cache.dtype)

    def products(pairs):
        for i in range(3):
            sums[i] = sum(
                dot_t(
                    jnp.concatenate([padded[r * cells : r * cells + tokens] for r in range(3)], axis=1),
                    jnp.concatenate([weights[back, row, i] for row in range(3)], axis=1),
                )
                for padded, back in [
                    (jnp.concatenate([ends, cache[frame], ends], axis=0), back) for frame, back in pairs
                ]
            )
        finished = []
        for start, row in ((tokens - cells, 0), (0, 2)):
            edge = jnp.concatenate([cache[frame, start : start + cells] for frame, _ in pairs], axis=1)
            parts = [
                dot_t(edge, jnp.concatenate([weights[back, row, i] for _, back in pairs], axis=1))
                for i in range(3)
            ]
            finished.append(gathered(parts, cells))
        up, down = finished
        even = lax.rem(place, 2) == 0
        pack(jnp.where(even, up, down), inner)
        pack(jnp.where(even, down, up), outer)

    @pl.when(moment == 0)
    def _():
        products([(0, 0), (1, 1)])

    @pl.when(moment == 1)
    def _():
        products([(1, 0)])

    @pl.when(moment > 1)
    def _():
        for out in (sums, inner, outer):
            out[...] = jnp.zeros_like(out)


def rest_kernel(cells, act, other, cached, keep, theirs, weights, out):
    parts = taps(by_core(act, other), weights.at[2], cells)
    terms = gathered([part + cached[i] for i, part in enumerate(parts)], cells)
    out[...] = by_core(keep, theirs).astype(F32) + terms


def edge_kernel(cells, rest, outer, inner, out):
    _, place, places, _ = place_of()
    tokens = rest.shape[0]
    even = lax.rem(place, 2) == 0
    above, below = jnp.where(even, outer[...], inner[...]), jnp.where(even, inner[...], outer[...])
    out[:cells] = rest[:cells] + jnp.where(place == 0, 0.0, unpacked(above))
    out[cells : tokens - cells] = rest[cells : tokens - cells]
    out[tokens - cells :] = rest[tokens - cells :] + jnp.where(place == places - 1, 0.0, unpacked(below))


def write(total, out, held, sem):
    held[...] = total.astype(BF)
    copy = pltpu.make_async_copy(held, out, sem)
    copy.start()
    copy.wait()


def early_kernel(rest, out, held, sem):
    @pl.when(place_of()[3] == 0)
    def _():
        write(rest[...], out, held, sem)


def final_kernel(rest, *refs):
    moment = place_of()[3]
    received, (_, out, held, sem) = refs[:-4], refs[-4:]

    @pl.when(moment > 0)
    def _():
        total = rest[...]
        for back, ref in enumerate(received):
            total = total + jnp.where(moment > back, unpacked(ref[...]), 0.0)
        write(total, out, held, sem)


def body(frames_in, cache, gain_one, gain_two, w_query, w_key, w_value, w_out, conv_weight):
    places, moments = lax.axis_size("space"), lax.axis_size("tm")
    _, rows, cells, half = frames_in.shape
    tokens, width = rows * cells, 2 * half
    count = tokens // 2 + cells

    gain = gain_one.reshape(1, width)
    gain_act = gain_two.reshape(1, width)
    weights = conv_weight.transpose(0, 1, 2, 4, 3)

    (packed,) = call(
        pack_kernel,
        [shaped((tokens * 3 // 2, LANES), BF)],
        [frames_in.reshape(tokens, half)],
        flops=4 * 10**9,
    )
    behind, ahead = cycle(packed, "space", 1), cycle(packed, "space", -1)
    cache = cache.reshape(2, tokens, width)
    own_other = between_cores(packed)
    raw_own, keys_own, query_own, w_query, w_key, w_mixed = call(
        own_rows_kernel,
        [
            shaped((tokens // 2, width), BF),
            shaped((tokens, width), BF),
            shaped((tokens // 2, width), BF),
            shaped((width, width), BF),
            shaped((width, width), BF),
            shaped((width, width), BF),
        ],
        [gain, packed, own_other, w_query, w_key, w_value, w_out],
        flops=1000,
    )
    raw_own, cache = lax.optimization_barrier((raw_own, cache))
    cached, inner, outer = call(
        functools.partial(cache_kernel, cells),
        [shaped((3, tokens, half), F32)] + [shaped((cells * 3 // 2, LANES), BF)] * 2,
        [cache, weights],
    )
    ahead, cached = lax.optimization_barrier((ahead, cached))
    ahead_other = between_cores(ahead)
    behind, ahead_other = lax.optimization_barrier((behind, ahead_other))
    tiles = [behind, between_cores(behind), ahead, ahead_other]
    up, down = behind, ahead
    groups = []
    for step in range(2, places // 2 + 1):
        down = cycle(down, "space", -1)
        if 2 * step < places:
            up = cycle(up, "space", 1)
            groups.append([up, down])
        else:
            groups.append([down])

    state = [
        shaped((count, LANES), F32),
        shaped((count, LANES), F32),
        shaped((count, width), F32),
    ]
    query, raw, top, total, accum = call(
        first_kernel,
        [shaped((count, width), BF), shaped((count, width), BF)] + state,
        [gain, raw_own, keys_own, query_own, w_query, w_key] + tiles,
        [pltpu.VMEM((3 * tokens, width), BF)],
    )
    for group in groups[:-1]:
        tiles = []
        for tile in group:
            tiles += [tile, cycle(tile, "chan", 1)]
        top, total, accum = call(
            functools.partial(middle_kernel, len(group)),
            state,
            [gain, query, top, total, accum] + tiles,
                )
    tile, accum = lax.optimization_barrier((groups[-1][0], accum))
    tile_other = cycle(tile, "chan", 1)
    act, joined = call(
        last_kernel,
        [shaped((count, width), BF)] * 2,
        [gain, gain_act, w_mixed, query, raw, top, total, accum, tile, tile_other],
        [pltpu.VMEM((count, 1), F32), pltpu.VMEM((count, width), F32)],
    )
    other = cycle(act, "chan", 1)
    keep, give = call(residual_kernel, [shaped((tokens // 2, half), BF)] * 2, [joined])
    other, give = lax.optimization_barrier((other, give))
    received = []
    for back in range(1, min(moments, 3)):
        (near,) = call(
            functools.partial(near_kernel, cells, back), [shaped((cells, half), F32)], [act, weights]
        )
        (term,) = call(
            functools.partial(send_kernel, cells, back),
            [shaped((tokens * 3 // 2, LANES), BF)],
            [near, act, other, weights],
            )
        received.append(term)
    act, give, received = lax.optimization_barrier((act, give, received))
    received = [cycle(term, "tm", 1 + i) for i, term in enumerate(received)]
    theirs = cycle(give, "chan", 1)
    (rest,) = call(
        functools.partial(rest_kernel, cells),
        [shaped((tokens, half), F32)],
        [act, other, cached, keep, theirs, weights],
    )
    inner, outer, act = lax.optimization_barrier((inner, outer, act))
    outer = lax.ppermute(
        outer, "space", [(i, min(max(((i + 1) ^ 1) - 1, 0), places - 1)) for i in range(places)]
    )
    inner = lax.ppermute(inner, "space", [(i, i ^ 1) for i in range(places)])
    (rest,) = call(
        functools.partial(edge_kernel, cells), [shaped((tokens, half), F32)], [rest, outer, inner]
    )
    written = [pltpu.VMEM((tokens, half), BF), pltpu.SemaphoreType.DMA]
    (out,) = call(early_kernel, [shaped((tokens, half), BF)], [rest], written, kept=True)
    (out,) = call(final_kernel, [shaped((tokens, half), BF)], [rest] + received + [out], written, kept=True)
    return out.reshape(1, rows, cells, half)


def solution(mesh):
    return jax.shard_map(
        body,
        mesh=mesh,
        in_specs=(
            P(("clips", "tm"), "space", None, "chan"),
            P("clips", "space", None, None),
            P(),
            P(),
            P(),
            P(),
            P(),
            P(),
            P(None, None, None, None, "chan"),
        ),
        out_specs=P(("clips", "tm"), "space", None, "chan"),
        check_vma=False,
    )
```

```python
import functools
import math
import jax
import jax.numpy as jnp
from jax import lax
from jax.experimental import pallas as pl
from jax.experimental.pallas import tpu as pltpu
from jax.sharding import PartitionSpec as P

EPS = 1e-06
LANES = 128
BF = jnp.bfloat16
F32 = jnp.float32


def cycle(array, axis, by):
    count = lax.axis_size(axis)
    return lax.ppermute(array, axis, [(i, (i + by) % count) for i in range(count)])


def between_cores(array, pieces=2):
    return jnp.concatenate([cycle(piece, "chan", 1) for piece in jnp.split(array, pieces)])


def call(kernel, outs, args, scratch=(), flops=1000, kept=False):
    vmem = pl.BlockSpec(memory_space=pltpu.VMEM)
    anywhere = pl.BlockSpec(memory_space=pl.ANY)
    into = kept and args[-1].shape == outs[0].shape and args[-1].dtype == outs[0].dtype
    return pl.pallas_call(
        kernel,
        out_shape=outs,
        in_specs=[vmem] * (len(args) - into) + [anywhere] * into,
        out_specs=[anywhere if kept else vmem] * len(outs),
        input_output_aliases={len(args) - 1: 0} if into else {},
        scratch_shapes=list(scratch),
        compiler_params=pltpu.CompilerParams(vmem_limit_bytes=36 * 2**20),
        cost_estimate=pl.CostEstimate(flops=flops, bytes_accessed=1000, transcendentals=0),
    )(*args)


def place_of():
    return lax.axis_index("chan"), lax.axis_index("space"), lax.axis_size("space"), lax.axis_index("tm")


def shaped(shape, dtype):
    return jax.ShapeDtypeStruct(shape, dtype)


def dot(a, b):
    return jnp.dot(a, b, preferred_element_type=F32)


def dot_t(a, b):
    return lax.dot_general(a, b, (((1,), (1,)), ((), ())), preferred_element_type=F32)


def pack(x, out):
    tokens = x.shape[0]
    out[:tokens, :] = x[:, :LANES].astype(BF)
    rest = x[:, LANES:]
    out[tokens:, :] = jnp.concatenate([rest[: tokens // 2], rest[tokens // 2 :]], axis=1).astype(BF)


def unpacked(packed):
    tokens = packed.shape[0] * 2 // 3
    rest = packed[tokens:].astype(F32)
    rest = jnp.concatenate([rest[:, : LANES // 2], rest[:, LANES // 2 :]], axis=0)
    return jnp.concatenate([packed[:tokens].astype(F32), rest], axis=1)


def pack_kernel(x, out):
    pack(x[...], out)


def joined_halves(core, mine, theirs):
    a, b = mine[...].astype(F32), theirs[...].astype(F32)
    first = jnp.where(core == 0, a, b)
    second = jnp.where(core == 0, b, a)
    tokens = a.shape[0] * 2 // 3
    turn = lambda v: pltpu.roll(v, LANES // 2, 1)
    low = lax.broadcasted_iota(jnp.int32, (tokens, LANES), 1) < LANES // 2
    middle = turn(second[:tokens])
    left = jnp.concatenate([first[tokens:], turn(first[tokens:])], axis=0)
    right = jnp.concatenate([turn(second[tokens:]), second[tokens:]], axis=0)
    return jnp.concatenate(
        [first[:tokens], jnp.where(low, left, middle), jnp.where(low, middle, right)], axis=1
    )


def rms_scaled(wide, gain):
    factor = lax.rsqrt(jnp.mean(wide * wide, axis=-1, keepdims=True) + EPS)
    return wide * factor * gain.astype(F32)


def attend(query, keys, top, total, accum):
    scores = [dot_t(query, k) for k in keys]
    new_top = top
    for s in scores:
        most = jnp.max(s, axis=-1, keepdims=True)
        new_top = most if new_top is None else jnp.maximum(new_top, most)
    if top is not None:
        fade = jnp.exp2(top - new_top)
        total, accum = total * fade, accum * fade
    for s, k in zip(scores, keys):
        weights = jnp.exp2(s - new_top)
        part = jnp.sum(weights, axis=-1, keepdims=True)
        mixed = dot(weights.astype(BF), k)
        total = part if total is None else total + part
        accum = mixed if accum is None else accum + mixed
    return new_top, total, accum


def queries(rows, w_query, w_key):
    scale = rows.shape[1] ** (-0.5) * math.log2(math.e)
    return (dot_t(dot(rows, w_query).astype(BF), w_key) * scale).astype(BF)


def own_rows_kernel(gain, mine, theirs, w_query, w_key, w_value, w_out, *refs):
    raw_out, keys_out, query_out, w_query_out, w_key_out, w_mixed_out = refs
    core = place_of()[0]
    raw = joined_halves(core, mine, theirs)
    half = raw.shape[0] // 2
    keys = rms_scaled(raw, gain[...]).astype(BF)
    keys_out[...] = keys
    raw_out[...] = jnp.where(core == 0, raw[:half], raw[half:]).astype(BF)
    rows = jnp.where(core == 0, keys[:half], keys[half:])
    query_out[...] = queries(rows, w_query[...], w_key[...])
    w_query_out[...] = w_query[...]
    w_key_out[...] = w_key[...]
    w_mixed_out[...] = dot(w_value[...], w_out[...]).astype(BF)


def first_kernel(gain, raw_own, keys_own, query_own, w_query, w_key, *refs):
    core = place_of()[0]
    tiles, (query_out, raw_out, top_out, total_out, accum_out, keys) = refs[:4], refs[4:]
    tokens = keys_own.shape[0]
    half = tokens // 2
    edge = raw_out.shape[0] - half
    behind, ahead = [joined_halves(core, tiles[2 * i], tiles[2 * i + 1]) for i in range(2)]
    keys[:tokens] = keys_own[...]
    keys[tokens : 2 * tokens] = rms_scaled(behind, gain[...]).astype(BF)
    keys[2 * tokens :] = rms_scaled(ahead, gain[...]).astype(BF)
    beyond = jnp.where(core == 0, behind[tokens - edge :], ahead[:edge])
    rows = jnp.where(core == 0, keys[2 * tokens - edge : 2 * tokens], keys[2 * tokens : 2 * tokens + edge])
    beyond = beyond.astype(BF)
    further = queries(rows, w_query[...], w_key[...])

    def ordered(own, other):
        return jnp.where(
            core == 0, jnp.concatenate([other, own], axis=0), jnp.concatenate([own, other], axis=0)
        )

    raw_out[...] = ordered(raw_own[...], beyond)
    query = ordered(query_own[...], further)
    query_out[...] = query
    top, total, accum = attend(query, [keys[...]], None, None, None)
    top_out[...] = jnp.broadcast_to(top, top_out.shape)
    total_out[...] = jnp.broadcast_to(total, total_out.shape)
    accum_out[...] = accum


def middle_kernel(count, gain, query, top, total, accum, *refs):
    core = place_of()[0]
    tiles, (top_out, total_out, accum_out) = refs[: 2 * count], refs[2 * count :]
    keys = [
        rms_scaled(joined_halves(core, tiles[2 * i], tiles[2 * i + 1]), gain[...]).astype(BF)
        for i in range(count)
    ]
    new = attend(query[...], keys, top[:, :1], total[:, :1], accum[...])
    top_out[...] = jnp.broadcast_to(new[0], top_out.shape)
    total_out[...] = jnp.broadcast_to(new[1], total_out.shape)
    accum_out[...] = new[2]


def last_kernel(gain, gain_two, w_mixed, query, raw, top, total, accum, mine, theirs, *refs):
    core, place, places, _ = place_of()
    act_out, joined_out, total_now, accum_now = refs
    keys = rms_scaled(joined_halves(core, mine, theirs), gain[...]).astype(BF)
    scores = dot_t(query[...], keys)
    weights = jnp.exp2(scores - top[:, :1])
    total_now[...] = total[:, :1] + jnp.sum(weights, axis=-1, keepdims=True)
    accum_now[...] = accum[...] + dot(weights.astype(BF), keys)

    @pl.when(jnp.max(jnp.max(scores, axis=-1, keepdims=True) - top[:, :1]) > 60.0)
    def _():
        _, total_now[...], accum_now[...] = attend(query[...], [keys], top[:, :1], total[:, :1], accum[...])

    mixed = (accum_now[...] * (1.0 / total_now[...])).astype(BF)
    joined = (raw[...].astype(F32) + dot(mixed, w_mixed[...])).astype(BF)
    joined_out[...] = joined
    edge = joined.shape[0] // 3
    act = rms_scaled(joined.astype(F32), gain_two[...])
    act = 0.5 * act
    act = act + act * jnp.tanh(act)
    row = lax.broadcasted_iota(jnp.int32, (act.shape[0], 1), 0)
    beyond = ((core == 0) & (place == 0) & (row < edge)) | (
        (core == 1) & (place == places - 1) & (row >= 2 * edge)
    )
    act_out[...] = jnp.where(beyond, 0.0, act).astype(BF)


def residual_kernel(joined, keep_out, give_out):
    core = place_of()[0]
    edge = joined.shape[0] // 3
    own = jnp.where(core == 0, joined[edge:], joined[: 2 * edge]).astype(F32)
    half = own.shape[1] // 2
    low, high = own[:, :half], own[:, half:]
    keep_out[...] = jnp.where(core == 0, low, high).astype(BF)
    give_out[...] = jnp.where(core == 0, high, low).astype(BF)


def taps(padded, weights, cells):
    tokens = padded.shape[0] - 2 * cells
    wide = jnp.concatenate([padded[i * cells : i * cells + tokens] for i in range(3)], axis=1)
    return [
        dot_t(wide, jnp.concatenate([weights[row, cell] for row in range(3)], axis=1))
        for cell in range(3)
    ]


def gathered(parts, cells):
    left, middle, right = parts
    tokens = middle.shape[0]
    cell = lax.rem(lax.broadcasted_iota(jnp.int32, (tokens, 1), 0), cells)
    left = jnp.where(cell == 0, 0.0, pltpu.roll(left, 1, 0))
    right = jnp.where(cell == cells - 1, 0.0, pltpu.roll(right, tokens - 1, 0))
    return middle + left + right


def by_core(mine, theirs):
    core, a, b = place_of()[0], mine[...], theirs[...]
    return jnp.concatenate([jnp.where(core == 0, a, b), jnp.where(core == 0, b, a)], axis=0)


def near_kernel(cells, back, act, weights, out):
    @pl.when(place_of()[3] + back < lax.axis_size("tm"))
    def _():
        out[...] = gathered(taps(act, weights.at[2 - back], cells), cells)


def send_kernel(cells, back, near, act, other, weights, out):
    wanted = place_of()[3] + back < lax.axis_size("tm")

    @pl.when(wanted)
    def _():
        core, mine, theirs = place_of()[0], act[...], other[...]
        own = mine.shape[0] - cells
        padded = jnp.where(
            core == 0,
            jnp.concatenate([mine[cells:], theirs], axis=0),
            jnp.concatenate([theirs, mine[:own]], axis=0),
        )
        rows = gathered(taps(padded, weights.at[2 - back], cells), cells)
        pack(jnp.concatenate([rows, near[...]], axis=0), out)

    @pl.when(jnp.logical_not(wanted))
    def _():
        out[...] = jnp.zeros_like(out)


def cache_kernel(cells, cache, weights, sums, inner, outer):
    _, place, _, moment = place_of()
    tokens = cache.shape[1]
    ends = jnp.zeros((cells, cache.shape[2]), cache.dtype)

    def products(pairs):
        for i in range(3):
            sums[i] = sum(
                dot_t(
                    jnp.concatenate([padded[r * cells : r * cells + tokens] for r in range(3)], axis=1),
                    jnp.concatenate([weights[back, row, i] for row in range(3)], axis=1),
                )
                for padded, back in [
                    (jnp.concatenate([ends, cache[frame], ends], axis=0), back) for frame, back in pairs
                ]
            )
        finished = []
        for start, row in ((tokens - cells, 0), (0, 2)):
            edge = jnp.concatenate([cache[frame, start : start + cells] for frame, _ in pairs], axis=1)
            parts = [
                dot_t(edge, jnp.concatenate([weights[back, row, i] for _, back in pairs], axis=1))
                for i in range(3)
            ]
            finished.append(gathered(parts, cells))
        up, down = finished
        even = lax.rem(place, 2) == 0
        pack(jnp.where(even, up, down), inner)
        pack(jnp.where(even, down, up), outer)

    @pl.when(moment == 0)
    def _():
        products([(0, 0), (1, 1)])

    @pl.when(moment == 1)
    def _():
        products([(1, 0)])

    @pl.when(moment > 1)
    def _():
        for out in (sums, inner, outer):
            out[...] = jnp.zeros_like(out)


def rest_kernel(cells, act, other, cached, keep, theirs, weights, out):
    parts = taps(by_core(act, other), weights.at[2], cells)
    terms = gathered([part + cached[i] for i, part in enumerate(parts)], cells)
    out[...] = by_core(keep, theirs).astype(F32) + terms


def edge_kernel(cells, rest, outer, inner, out):
    _, place, places, _ = place_of()
    tokens = rest.shape[0]
    even = lax.rem(place, 2) == 0
    above, below = jnp.where(even, outer[...], inner[...]), jnp.where(even, inner[...], outer[...])
    out[:cells] = rest[:cells] + jnp.where(place == 0, 0.0, unpacked(above))
    out[cells : tokens - cells] = rest[cells : tokens - cells]
    out[tokens - cells :] = rest[tokens - cells :] + jnp.where(place == places - 1, 0.0, unpacked(below))


def write(total, out, held, sem):
    held[...] = total.astype(BF)
    copy = pltpu.make_async_copy(held, out, sem)
    copy.start()
    copy.wait()


def early_kernel(rest, out, held, sem):
    @pl.when(place_of()[3] == 0)
    def _():
        write(rest[...], out, held, sem)


def final_kernel(cells, rest, *refs):
    moment = place_of()[3]
    received, (_, out, held, sem) = refs[:-4], refs[-4:]

    @pl.when(moment > 0)
    def _():
        total = rest[...]
        for back, ref in enumerate(received):
            term = unpacked(ref[...])
            own = term.shape[0] - cells
            ordered = jnp.concatenate([term[own:], term[:own]], axis=0)
            term = jnp.where(place_of()[0] == 0, ordered, term)
            total = total + jnp.where(moment > back, term, 0.0)
        write(total, out, held, sem)


def body(frames_in, cache, gain_one, gain_two, w_query, w_key, w_value, w_out, conv_weight):
    places, moments = lax.axis_size("space"), lax.axis_size("tm")
    _, rows, cells, half = frames_in.shape
    tokens, width = rows * cells, 2 * half
    count = tokens // 2 + cells

    gain = gain_one.reshape(1, width)
    gain_act = gain_two.reshape(1, width)
    weights = conv_weight.transpose(0, 1, 2, 4, 3)

    (packed,) = call(
        pack_kernel,
        [shaped((tokens * 3 // 2, LANES), BF)],
        [frames_in.reshape(tokens, half)],
        flops=4 * 10**9,
    )
    behind, ahead = cycle(packed, "space", 1), cycle(packed, "space", -1)
    cache = cache.reshape(2, tokens, width)
    own_other = between_cores(packed)
    raw_own, keys_own, query_own, w_query, w_key, w_mixed = call(
        own_rows_kernel,
        [
            shaped((tokens // 2, width), BF),
            shaped((tokens, width), BF),
            shaped((tokens // 2, width), BF),
            shaped((width, width), BF),
            shaped((width, width), BF),
            shaped((width, width), BF),
        ],
        [gain, packed, own_other, w_query, w_key, w_value, w_out],
        flops=1000,
    )
    raw_own, cache = lax.optimization_barrier((raw_own, cache))
    cached, inner, outer = call(
        functools.partial(cache_kernel, cells),
        [shaped((3, tokens, half), F32)] + [shaped((cells * 3 // 2, LANES), BF)] * 2,
        [cache, weights],
    )
    ahead, cached = lax.optimization_barrier((ahead, cached))
    ahead_other = between_cores(ahead)
    behind, ahead_other = lax.optimization_barrier((behind, ahead_other))
    tiles = [behind, between_cores(behind), ahead, ahead_other]
    up, down = behind, ahead
    groups = []
    for step in range(2, places // 2 + 1):
        down = cycle(down, "space", -1)
        if 2 * step < places:
            up = cycle(up, "space", 1)
            groups.append([up, down])
        else:
            groups.append([down])

    state = [
        shaped((count, LANES), F32),
        shaped((count, LANES), F32),
        shaped((count, width), F32),
    ]
    query, raw, top, total, accum = call(
        first_kernel,
        [shaped((count, width), BF), shaped((count, width), BF)] + state,
        [gain, raw_own, keys_own, query_own, w_query, w_key] + tiles,
        [pltpu.VMEM((3 * tokens, width), BF)],
    )
    for group in groups[:-1]:
        tiles = []
        for tile in group:
            tiles += [tile, cycle(tile, "chan", 1)]
        top, total, accum = call(
            functools.partial(middle_kernel, len(group)),
            state,
            [gain, query, top, total, accum] + tiles,
                )
    tile, accum = lax.optimization_barrier((groups[-1][0], accum))
    tile_other = cycle(tile, "chan", 1)
    act, joined = call(
        last_kernel,
        [shaped((count, width), BF)] * 2,
        [gain, gain_act, w_mixed, query, raw, top, total, accum, tile, tile_other],
        [pltpu.VMEM((count, 1), F32), pltpu.VMEM((count, width), F32)],
    )
    other = cycle(act, "chan", 1)
    keep, give = call(residual_kernel, [shaped((tokens // 2, half), BF)] * 2, [joined])
    other, give = lax.optimization_barrier((other, give))
    received = []
    for back in range(1, min(moments, 3)):
        (near,) = call(
            functools.partial(near_kernel, cells, back), [shaped((cells, half), F32)], [act, weights]
        )
        (term,) = call(
            functools.partial(send_kernel, cells, back),
            [shaped((tokens * 3 // 2, LANES), BF)],
            [near, act, other, weights],
            )
        received.append(term)
    act, give, received = lax.optimization_barrier((act, give, received))
    received = [cycle(term, "tm", 1 + i) for i, term in enumerate(received)]
    theirs = cycle(give, "chan", 1)
    (rest,) = call(
        functools.partial(rest_kernel, cells),
        [shaped((tokens, half), F32)],
        [act, other, cached, keep, theirs, weights],
    )
    inner, outer, act = lax.optimization_barrier((inner, outer, act))
    outer = lax.ppermute(
        outer, "space", [(i, min(max(((i + 1) ^ 1) - 1, 0), places - 1)) for i in range(places)]
    )
    inner = lax.ppermute(inner, "space", [(i, i ^ 1) for i in range(places)])
    (rest,) = call(
        functools.partial(edge_kernel, cells), [shaped((tokens, half), F32)], [rest, outer, inner]
    )
    written = [pltpu.VMEM((tokens, half), BF), pltpu.SemaphoreType.DMA]
    (out,) = call(early_kernel, [shaped((tokens, half), BF)], [rest], written, kept=True)
    (out,) = call(
        functools.partial(final_kernel, cells), [shaped((tokens, half), BF)], [rest] + received + [out], written, kept=True
    )
    return out.reshape(1, rows, cells, half)


def solution(mesh):
    return jax.shard_map(
        body,
        mesh=mesh,
        in_specs=(
            P(("clips", "tm"), "space", None, "chan"),
            P("clips", "space", None, None),
            P(),
            P(),
            P(),
            P(),
            P(),
            P(),
            P(None, None, None, None, "chan"),
        ),
        out_specs=P(("clips", "tm"), "space", None, "chan"),
        check_vma=False,
    )
```
